256 devices in a mesh: gx: 64 (over z, y, core), gy: 4 (over x).
Axes of the slice: x: 4, y: 4, z: 8, core: 2. Of those that a mesh axis runs over, the one named last changes fastest.
Arguments:
- rhs_field: bfloat16 [128, 8, 2, 320, 128], P('gx', 'gy'), may hold values from -6 to 6
- inv_block: bfloat16 [128, 8, 2, 320, 320], P('gx', 'gy'), may hold values from -0.3125 to 0.3125
- face_block: bfloat16 [128, 8, 2, 6, 80, 80], P('gx', 'gy'), may hold values from -0.625 to 0.625
- hang_list: int32 [64, 4, 32, 4], P('gx', 'gy'), may hold values from -1 to 7, as said below
- hang_count: int32 [64, 4], P('gx', 'gy'), may hold values from 8 to 32, as said below
- hang_block: bfloat16 [64, 4, 32, 80, 320], P('gx', 'gy'), may hold values from -0.625 to 0.625
Outputs:
- basis_last: float32 [128, 8, 2, 320, 128], P('gx', 'gy')
- hessenberg: float32 [3, 2, 128], replicated
The draws below stay inside these ranges and needn't reach their ends.
Inputs may be any that keep to these rules, and one draw needn't show every extreme that they name: `hang_list`: Columns: fine element 0 to 7, face 0 to 5, offset -1, 0 or 1 and never past the ends of gx, owner 0 to 7. `hang_count`: some device holds 32 live couplings in every draw.
All inputs are finite; a program needn't handle non-finite values.
Results may differ from the reference program's by a relative error of at most 0.0065.
Values may be sent and summed in bfloat16 or wider, within the bound.
No kernel may reach another device: no remote copies, remote signals or barrier semaphores. Data moves between devices by JAX's collectives and lax.ppermute only.
A program may use at most 128 MiB of HBM per device.

```python
import jax
import jax.numpy as jnp
from jax import lax

VARS = 5
NP = 4
BLOCK = 320
FACE = 80
EX = 2
EY = 2
EZ = 2
RHS = 128
HANG = 32
ITERS = 2
NXE = 128
NYE = 8
N_GX = 64
N_GY = 4


def draw_hang_list(key, part):
    key = jax.random.fold_in(key, 11)
    keys = jax.random.split(key, 4)
    shape = (N_GX, N_GY, HANG)
    element = jax.random.randint(keys[0], shape, 0, EX * EY * EZ)
    facing = jax.random.randint(keys[1], shape, 0, 6)
    moving = jax.random.randint(keys[2], shape, -1, 2)
    row_index = jnp.arange(N_GX)[:, None, None] + jnp.zeros(shape, jnp.int32)
    moving = jnp.where((row_index + moving < 0) | (row_index + moving >= N_GX), 0, moving)
    owning = jax.random.randint(keys[3], shape, 0, EX * EY * EZ)
    return jnp.stack([element, facing, moving, owning], axis=-1).astype(jnp.int32)


def draw_hang_count(key, part):
    key = jax.random.fold_in(key, 23)
    keys = jax.random.split(key, 2)
    counts = jax.random.randint(keys[0], (N_GX * N_GY,), max(1, HANG // 4), HANG + 1)
    chosen = jax.random.randint(keys[1], (), 0, N_GX * N_GY)
    counts = jnp.where(jnp.arange(N_GX * N_GY) == chosen, HANG, counts)
    return counts.reshape(N_GX, N_GY).astype(jnp.int32)


def block_levels(rng, extent, cuts, smallest, high):
    level = 1.0
    for axis_at, shards_of in cuts:
        heights = jax.random.uniform(jax.random.fold_in(jax.random.fold_in(rng, 6), axis_at), (shards_of,), jnp.float32, smallest / len(cuts), high / len(cuts))
        level = level * jnp.repeat(jnp.exp(heights), extent[axis_at] // shards_of).reshape((-1,) + (1,) * (len(extent) - 1 - axis_at))
    return level


def bell_draw(stream_key, dims, deviation, limit, cuts=(), held_as=jnp.bfloat16):
    gain = block_levels(stream_key, dims, cuts, -0.22, 0.18) if cuts else 1.0
    values = jax.random.normal(stream_key, dims, jnp.float32) * deviation * gain
    return jnp.minimum(jnp.maximum(values, -limit), limit).astype(held_as)


def setup_inputs(seed: int = 0) -> dict:
    splits = jax.random.split(jax.random.key(seed), 7)
    return {
        "rhs_field": bell_draw(splits[0], (NXE, NYE, EZ, BLOCK, RHS), 1.0, 6.0, ((0, 64), (1, 4))),
        "inv_block": bell_draw(splits[1], (NXE, NYE, EZ, BLOCK, BLOCK), BLOCK ** -0.5, 0.3125, ((0, 64), (1, 4))),
        "face_block": bell_draw(splits[2], (NXE, NYE, EZ, 6, FACE, FACE), FACE ** -0.5, 0.625, ((0, 64), (1, 4))),
        "hang_list": draw_hang_list(jax.random.fold_in(splits[6], 71), 0),
        "hang_count": draw_hang_count(jax.random.fold_in(splits[6], 71), 0),
        "hang_block": bell_draw(splits[5], (N_GX, N_GY, HANG, FACE, BLOCK), FACE ** -0.5, 0.625, ((0, 64), (1, 4))),
    }


def face_traces(field):
    size_x, size_y, size_z = field.shape[:3]
    columns = field.shape[-1]
    cube = field.reshape(size_x, size_y, size_z, VARS, NP, NP, NP, columns)
    pieces = [cube[:, :, :, :, 0], cube[:, :, :, :, NP - 1], cube[:, :, :, :, :, 0], cube[:, :, :, :, :, NP - 1], cube[:, :, :, :, :, :, 0], cube[:, :, :, :, :, :, NP - 1]]
    return jnp.stack([piece.reshape(size_x, size_y, size_z, VARS * NP * NP, columns) for piece in pieces], axis=3)

def place_faces(landed):
    size_x, size_y, size_z = landed[0].shape[:3]
    columns = landed[0].shape[-1]
    total = jnp.zeros((size_x, size_y, size_z, VARS, NP, NP, NP, columns), jnp.float32)
    for face in range(6):
        direction = face // 2
        shape = [VARS, NP, NP, NP]
        shape[1 + direction] = 1
        piece = landed[face].reshape((size_x, size_y, size_z) + tuple(shape) + (columns,))
        widths = [(0, 0)] * 8
        widths[4 + direction] = (0, NP - 1) if face % 2 == 0 else (NP - 1, 0)
        total = total + jnp.pad(piece, widths)
    return total.reshape(size_x, size_y, size_z, VARS * NP ** 3, columns)

def slide(values, axis, forward):
    length = values.shape[axis]
    widths = [(0, 0)] * values.ndim
    if forward:
        kept = lax.slice_in_dim(values, 0, length - 1, axis=axis)
        widths[axis] = (1, 0)
    else:
        kept = lax.slice_in_dim(values, 1, length, axis=axis)
        widths[axis] = (0, 1)
    return jnp.pad(kept, widths)

def apply_operator(field, inv_block, face_block, hang_list, hang_count, hang_block):
    lowered = field.astype(jnp.bfloat16)

    def precondition(pair):
        blocks, values = pair
        return jnp.einsum('yzij,yzir->yzjr', blocks.astype(jnp.float32), values.astype(jnp.float32)).astype(jnp.bfloat16)
    applied = lax.map(precondition, (inv_block, lowered))
    traces = face_traces(applied)

    def couple(pair):
        blocks, values = pair
        return jnp.einsum('yzfkl,yzfkr->yzflr', blocks.astype(jnp.float32), values.astype(jnp.float32))
    flux = lax.map(couple, (face_block, traces))
    landed = [slide(flux[:, :, :, 1], 0, True), slide(flux[:, :, :, 0], 0, False), slide(flux[:, :, :, 3], 1, True), slide(flux[:, :, :, 2], 1, False), slide(flux[:, :, :, 5], 2, True), slide(flux[:, :, :, 4], 2, False)]
    result = field + place_faces(landed)
    elems = EX * EY * EZ
    columns = field.shape[-1]
    per_device = traces.reshape(N_GX, EX, N_GY, EY, EZ, 6, FACE, columns).transpose(0, 2, 1, 3, 4, 5, 6, 7).reshape(N_GX, N_GY, elems * 6, FACE, columns)
    source = (hang_list[:, :, :, 0] * 6 + hang_list[:, :, :, 1]).astype(jnp.int32)
    chosen = jnp.take_along_axis(per_device, source[:, :, :, None, None], axis=2)
    live = (jnp.arange(HANG).astype(jnp.int32)[None, None, :] < hang_count[:, :, None]).astype(jnp.float32)
    contrib = jnp.einsum('abhkj,abhkr->abhjr', hang_block.astype(jnp.float32), chosen.astype(jnp.float32)) * live[:, :, :, None, None]
    device_row = jnp.arange(N_GX).astype(jnp.int32)[:, None, None] + hang_list[:, :, :, 2]
    target = ((device_row * N_GY + jnp.arange(N_GY).astype(jnp.int32)[None, :, None]) * elems + hang_list[:, :, :, 3]).astype(jnp.int32)
    summed = jax.ops.segment_sum(contrib.reshape(-1, BLOCK, columns), target.reshape(-1), num_segments=N_GX * N_GY * elems)
    summed = summed.reshape(N_GX, N_GY, EX, EY, EZ, BLOCK, columns).transpose(0, 2, 1, 3, 4, 5, 6).reshape(N_GX * EX, N_GY * EY, EZ, BLOCK, columns)
    return result + summed

def reference(rhs_field, inv_block, face_block, hang_list, hang_count, hang_block):
    start = rhs_field.astype(jnp.float32)
    entries = float(NXE * NYE * EZ * BLOCK)
    basis = [start / jnp.sqrt(lax.optimization_barrier(jnp.sum(start * start, axis=(0, 1, 2, 3))) / entries + 1e-06)]
    hessenberg = jnp.zeros((ITERS + 1, ITERS, start.shape[-1]), jnp.float32)
    for iteration in range(ITERS):
        image = apply_operator(basis[-1], inv_block, face_block, hang_list, hang_count, hang_block)
        stacked = jnp.stack(basis)
        inner = lax.optimization_barrier(jnp.sum(stacked * image[None], axis=(1, 2, 3, 4))) / entries
        image = image - lax.optimization_barrier(jnp.sum(inner[:, None, None, None, None, :] * stacked, axis=0))
        scale = jnp.sqrt(lax.optimization_barrier(jnp.sum(image * image, axis=(0, 1, 2, 3))) / entries + 1e-06)
        hessenberg = hessenberg.at[:iteration + 1, iteration].set(inner).at[iteration + 1, iteration].set(scale)
        basis.append(image / scale)
    return (basis[-1], hessenberg)
```

```python
import functools

import jax
import jax.numpy as jnp
from jax import lax
from jax.experimental import pallas as pl
from jax.experimental.pallas import tpu as pltpu
from jax.sharding import PartitionSpec as P

VARS = 5
NP = 4
BLOCK = 320
FACE = 80
ELEMS = 8
RHS = 128
HANG = 32
EPS = 1e-6
GROUP = 2
VMEM_LIMIT = 40 * 1024 * 1024

TN = (((0,), (0,)), ((), ()))
NN = (((1,), (0,)), ((), ()))


def mm(a, b, dims):
    return lax.dot_general(a, b, dims, preferred_element_type=jnp.float32)


def select_matrix():
    row = lax.broadcasted_iota(jnp.int32, (4 * FACE, BLOCK), 0)
    col = lax.broadcasted_iota(jnp.int32, (4 * FACE, BLOCK), 1)
    group = (
        (row >= FACE).astype(jnp.int32)
        + (row >= 2 * FACE).astype(jnp.int32)
        + (row >= 3 * FACE).astype(jnp.int32)
    )
    entry = row - group * FACE
    along_b = lax.shift_right_logical(entry, 2) * 16 + (entry & 3) + 12 * (group & 1)
    along_c = entry * 4 + 3 * (group & 1)
    source = jnp.where(group < 2, along_b, along_c)
    return (source == col).astype(jnp.float32).astype(jnp.bfloat16)


def fill_traces(lowered, inv_ref, tr_ref):
    pick = select_matrix()
    for e in range(ELEMS):
        applied = mm(inv_ref[e], lowered(e), TN).astype(jnp.bfloat16)
        for v in range(VARS):
            tr_ref[6 * e, 16 * v : 16 * v + 16, :] = applied[64 * v : 64 * v + 16]
            tr_ref[6 * e + 1, 16 * v : 16 * v + 16, :] = applied[64 * v + 48 : 64 * v + 64]
        others = mm(pick, applied, NN).astype(jnp.bfloat16)
        for g in range(4):
            tr_ref[6 * e + 2 + g] = others[FACE * g : FACE * g + FACE]


def flux(face_ref, tr_ref, e, f):
    return mm(face_ref[6 * e + f], tr_ref[6 * e + f], TN)


def add_face(acc, e, f, values, tmp):
    end = f % 2
    if f < 2:
        for v in range(VARS):
            first = 64 * v + 48 * end
            acc[e, first : first + 16, :] += values[16 * v : 16 * v + 16]
    elif f < 4:
        tmp[...] = values
        for c in range(NP):
            at = pl.ds(12 * end + c, 20, stride=16)
            acc[e, at, :] += tmp[pl.ds(c, 20, stride=4), :]
    else:
        acc[e, pl.ds(3 * end, FACE, stride=4), :] += values


def add_slots(acc, wanted, sign, list_ref, count_ref, hang_ref, tr_ref, slot_ref):
    live = count_ref[0]

    def look(h, n):
        slot_ref[n] = h
        hit = jnp.logical_and(list_ref[h, 2] * sign == wanted, h < live)
        return n + hit.astype(jnp.int32)

    n = lax.fori_loop(0, HANG, look, jnp.int32(0))
    for i in range(GROUP):
        slot_ref[n + i] = 0

    def work(g, carry):
        parts = []
        for i in range(GROUP):
            k = g * GROUP + i
            h = slot_ref[k]
            source = list_ref[h, 0] * 6 + list_ref[h, 1]
            target = jnp.where(k < n, list_ref[h, 3], ELEMS)
            parts.append((target, mm(hang_ref[h], tr_ref[source], TN)))
        for target, part in parts:
            acc[target] += part
        return carry

    lax.fori_loop(0, (n + GROUP - 1) // GROUP, work, 0)


def core_and_row():
    return lax.axis_index("c"), lax.axis_index("x") % 2


def outgoing_x(side, acc, face_ref, tr_ref):
    for n in range(4):
        acc_e = n + 4 * (1 - side)
        add_face(acc, acc_e, 1 - side, flux(face_ref, tr_ref, n + 4 * side, side), None)


def cross_part(acc, out_ref, list_ref, count_ref, face_ref, hang_ref, tr_ref, slot_ref, wanted):
    core, _ = core_and_row()
    acc[...] = jnp.zeros_like(acc)
    side = core if wanted == 1 else 1 - core
    for s in range(2):

        @pl.when(side == s)
        def _(s=s):
            outgoing_x(s, acc, face_ref, tr_ref)

    add_slots(acc, wanted, 2 * core - 1, list_ref, count_ref, hang_ref, tr_ref, slot_ref)
    out_ref[...] = acc[0:ELEMS].astype(out_ref.dtype)


def first_kernel(list_ref, count_ref, rhs_ref, inv_ref, face_ref, hang_ref, tr_ref, cross_ref, acc, slot_ref):
    fill_traces(lambda e: rhs_ref[e], inv_ref, tr_ref)
    cross_part(acc, cross_ref, list_ref, count_ref, face_ref, hang_ref, tr_ref, slot_ref, 1)


def side_kernel(list_ref, count_ref, face_ref, hang_ref, tr_ref, chip_ref, ya_ref, yb_ref, acc, slot_ref):
    _, odd = core_and_row()
    for parity in range(2):

        @pl.when(odd == parity)
        def _(parity=parity):
            for x in range(2):
                for z in range(2):
                    up = 4 * x + 2 + z
                    down = 4 * x + z
                    refs = (ya_ref, yb_ref) if parity == 0 else (yb_ref, ya_ref)
                    refs[0][2 * x + z] = flux(face_ref, tr_ref, up, 3)
                    refs[1][2 * x + z] = flux(face_ref, tr_ref, down, 2)

    cross_part(acc, chip_ref, list_ref, count_ref, face_ref, hang_ref, tr_ref, slot_ref, -1)


def own_body(list_ref, count_ref, face_ref, hang_ref, tr_ref, own_ref, acc, tmp, slot_ref):
    acc[...] = jnp.zeros_like(acc)
    for direction, step in ((0, 4), (1, 2), (2, 1)):
        for e in range(ELEMS):
            low, high = 2 * direction, 2 * direction + 1
            if e & step:
                add_face(acc, e - step, high, flux(face_ref, tr_ref, e, low), tmp)
            else:
                add_face(acc, e + step, low, flux(face_ref, tr_ref, e, high), tmp)
    core, _ = core_and_row()
    add_slots(acc, 0, 1, list_ref, count_ref, hang_ref, tr_ref, slot_ref)
    own_ref[...] = acc[0:ELEMS]


def own_kernel(list_ref, count_ref, face_ref, hang_ref, tr_ref, own_ref, acc, tmp, slot_ref):
    own_body(list_ref, count_ref, face_ref, hang_ref, tr_ref, own_ref, acc, tmp, slot_ref)


def own_gram_kernel(
    list_ref, count_ref, face_ref, hang_ref, tr_ref, rhs_ref, w1_ref, own_ref, gram_ref, acc, tmp, slot_ref
):
    own_body(list_ref, count_ref, face_ref, hang_ref, tr_ref, own_ref, acc, tmp, slot_ref)
    zero = jnp.zeros((8, RHS), jnp.float32)
    g00, g01, g11 = zero, zero, zero
    for e in range(ELEMS):
        a = rhs_ref[e].astype(jnp.float32).reshape(BLOCK // 8, 8, RHS)
        b = w1_ref[e].reshape(BLOCK // 8, 8, RHS)
        g00 += jnp.sum(a * a, axis=0)
        g01 += jnp.sum(a * b, axis=0)
        g11 += jnp.sum(b * b, axis=0)
    rows = [jnp.sum(g, axis=0, keepdims=True) for g in (g00, g01, g11)]
    gram_ref[...] = jnp.concatenate(rows + [jnp.zeros((5, RHS), jnp.float32)], axis=0)


def land(w_ref, own_ref, cross_ref, chip_ref, ya_ref, yb_ref):
    w_ref[...] = own_ref[...] + cross_ref[...].astype(jnp.float32) + chip_ref[...].astype(jnp.float32)
    _, odd = core_and_row()
    for parity in range(2):

        @pl.when(odd == parity)
        def _(parity=parity):
            from_up, from_down = (ya_ref, yb_ref) if parity == 0 else (yb_ref, ya_ref)
            for x in range(2):
                for z in range(2):
                    n = 2 * x + z
                    for c in range(NP):
                        rows = pl.ds(c, 20, stride=4)
                        high = pl.ds(12 + c, 20, stride=16)
                        low = pl.ds(c, 20, stride=16)
                        w_ref[4 * x + 2 + z, high, :] += from_up[n, rows, :]
                        w_ref[4 * x + z, low, :] += from_down[n, rows, :]


def second_kernel(
    list_ref, count_ref, own_ref, in_cross, in_chip, in_ya, in_yb, inv_ref, face_ref, hang_ref,
    w_ref, tr_ref, cross_ref, acc, slot_ref,
):
    land(w_ref, own_ref, in_cross, in_chip, in_ya, in_yb)
    fill_traces(lambda e: w_ref[e].astype(jnp.bfloat16), inv_ref, tr_ref)
    cross_part(acc, cross_ref, list_ref, count_ref, face_ref, hang_ref, tr_ref, slot_ref, 1)


def last_kernel(own_ref, in_cross, in_chip, in_ya, in_yb, rhs_ref, w1_ref, early_ref, w_ref, gram_ref):
    land(w_ref, own_ref, in_cross, in_chip, in_ya, in_yb)
    zero = jnp.zeros((8, RHS), jnp.float32)
    g02, g12, g22 = zero, zero, zero
    for e in range(ELEMS):
        a = rhs_ref[e].astype(jnp.float32).reshape(BLOCK // 8, 8, RHS)
        b = w1_ref[e].reshape(BLOCK // 8, 8, RHS)
        c = w_ref[e].reshape(BLOCK // 8, 8, RHS)
        g02 += jnp.sum(a * c, axis=0)
        g12 += jnp.sum(b * c, axis=0)
        g22 += jnp.sum(c * c, axis=0)
    rows = [jnp.sum(g, axis=0, keepdims=True) for g in (g02, g12, g22)]
    gram_ref[...] = jnp.concatenate(
        [early_ref[0:3]] + rows + [jnp.zeros((2, RHS), jnp.float32)], axis=0
    )


def combine_kernel(entries, sums_ref, rhs_ref, w1_ref, w2_ref, out_ref, hess_ref):
    gram = jnp.sum(sums_ref[...], axis=0) * (1.0 / entries)
    g00, g01, g11, g02, g12, g22 = (gram[i : i + 1] for i in range(6))
    norm0 = g00 + EPS
    size0 = jnp.sqrt(norm0)
    h11 = (g00 + g01) / norm0
    c1 = (EPS - g01) / norm0
    square1 = jnp.maximum(g11 + 2.0 * c1 * g01 + c1 * c1 * g00, 0.0) / norm0 + EPS
    h21 = jnp.sqrt(square1)
    s2 = 1.0 / (size0 * h21)
    ratio = (g02 + c1 * g01 + EPS * h11) / norm0
    h12 = ratio * s2 * size0
    q = EPS / square1 - s2 * s2 * (g12 + c1 * (g11 + g02 + c1 * g01))
    h22 = 1.0 - q
    alpha = c1 + q
    beta = c1 * q - ratio
    total = g22 + 2.0 * (alpha * g12 + beta * g02 + alpha * beta * g01)
    total = total + alpha * alpha * g11 + beta * beta * g00
    h32 = jnp.sqrt(s2 * s2 * jnp.maximum(total, 0.0) + EPS)
    zero = jnp.zeros_like(h11)
    for i, row in enumerate(((h11, h12), (h21, h22), (zero, h32))):
        hess_ref[i] = jnp.concatenate(row, axis=0)
    k2 = s2 / h32
    k1 = k2 * alpha
    k0 = k2 * beta
    for e in range(ELEMS):
        out_ref[e] = k2 * w2_ref[e] + k1 * w1_ref[e] + k0 * rhs_ref[e].astype(jnp.float32)


def shape(dims, dtype=jnp.float32):
    return jax.ShapeDtypeStruct(dims, dtype)


FIELD = (ELEMS, BLOCK, RHS)
TRACES = (6 * ELEMS, FACE, RHS)
SIDE = (4, FACE, RHS)
SMEM = pl.BlockSpec(memory_space=pltpu.SMEM)
VMEM = pl.BlockSpec(memory_space=pltpu.VMEM)


def call(kernel, n_smem, n_vmem, outs, scratch, flops, moved):
    return pl.pallas_call(
        kernel,
        out_shape=outs,
        in_specs=[SMEM] * n_smem + [VMEM] * n_vmem,
        out_specs=[VMEM] * len(outs),
        scratch_shapes=scratch,
        compiler_params=pltpu.CompilerParams(vmem_limit_bytes=VMEM_LIMIT),
        cost_estimate=pl.CostEstimate(flops=flops, bytes_accessed=moved, transcendentals=0),
    )


def per_device(entries, pairs, rhs_field, inv_block, face_block, hang_list, hang_count, hang_block):
    rhs = rhs_field.reshape(FIELD)
    inv = inv_block.reshape(ELEMS, BLOCK, BLOCK)
    face = face_block.reshape(6 * ELEMS, FACE, FACE)
    hang = hang_block.reshape(HANG, FACE, BLOCK)
    rows = hang_list.reshape(HANG, 4)
    count = hang_count.reshape(1)
    acc = pltpu.VMEM((ELEMS + 1, BLOCK, RHS), jnp.float32)
    tmp = pltpu.VMEM((FACE, RHS), jnp.float32)
    slots = pltpu.SMEM((HANG + 8,), jnp.int32)
    bf16 = jnp.bfloat16
    million = 10**6

    def exchange(traces, cross, own_call):
        in_cross = lax.ppermute(cross, ("z", "y", "c"), pairs["cross"])
        chip, ya, yb = call(
            side_kernel, 2, 3, [shape(FIELD, bf16), shape(SIDE), shape(SIDE)], [acc, slots],
            100 * million, 4 * million,
        )(rows, count, face, hang, traces)
        in_chip = lax.ppermute(chip, "c", [(0, 1), (1, 0)])
        in_ya = lax.ppermute(ya, "x", pairs["even"])
        in_yb = lax.ppermute(yb, "x", pairs["odd"])
        return own_call(traces), (in_cross, in_chip, in_ya, in_yb)

    traces, cross = call(
        first_kernel, 2, 4, [shape(TRACES, bf16), shape(FIELD, bf16)], [acc, slots],
        300 * million, 6 * million,
    )(rows, count, rhs, inv, face, hang)

    def own_first(traces):
        return call(
            own_kernel, 2, 3, [shape(FIELD)], [acc, tmp, slots], 100 * million, 6 * million
        )(rows, count, face, hang, traces)[0]

    own, arrived = exchange(traces, cross, own_first)
    w1, traces, cross = call(
        second_kernel, 2, 8, [shape(FIELD), shape(TRACES, bf16), shape(FIELD, bf16)], [acc, slots],
        300 * million, 8 * million,
    )(rows, count, own, *arrived, inv, face, hang)

    def own_second(traces):
        return call(
            own_gram_kernel, 2, 5, [shape(FIELD), shape((8, RHS))], [acc, tmp, slots],
            100 * million, 6 * million,
        )(rows, count, face, hang, traces, rhs, w1)

    (own, early), arrived = exchange(traces, cross, own_second)
    w2, gram = call(
        last_kernel, 0, 8, [shape(FIELD), shape((8, RHS))], [], 10 * million, 8 * million
    )(own, *arrived, rhs, w1, early)

    gram = gram + lax.ppermute(gram, "c", [(0, 1), (1, 0)])
    chips = lax.axis_size(("z", "y", "x"))
    sums = lax.all_to_all(jnp.broadcast_to(gram, (chips, 8, RHS)), ("z", "y", "x"), 0, 0)
    last, hessenberg = call(
        functools.partial(combine_kernel, entries), 0, 4, [shape(FIELD), shape((3, 2, RHS))], [],
        10 * million, 6 * million,
    )(sums, rhs, w1, w2)
    return last.reshape(rhs_field.shape), hessenberg


def solution(mesh):
    count_x, count_y = mesh.shape["gx"], mesh.shape["gy"]
    grid = jax.sharding.Mesh(
        mesh.devices.reshape(count_x // 8, 4, 2, count_y), ("z", "y", "c", "x")
    )
    pairs = {"cross": [], "even": [], "odd": []}
    for i in range(1, count_x - 1, 2):
        pairs["cross"] += [(i, i + 1), (i + 1, i)]
    for j in range(count_y - 1):
        pairs["odd" if j % 2 else "even"] += [(j, j + 1), (j + 1, j)]
    long = ("z", "y", "c")
    in_specs = (P(long, "x"),) * 6
    out_specs = (P(long, "x"), P())
    entries = float(ELEMS * BLOCK * count_x * count_y)
    return jax.shard_map(
        functools.partial(per_device, entries, pairs),
        mesh=grid, in_specs=in_specs, out_specs=out_specs, check_vma=False,
    )
```

```python
import functools

import jax
import jax.numpy as jnp
from jax import lax
from jax.experimental import pallas as pl
from jax.experimental.pallas import tpu as pltpu
from jax.sharding import PartitionSpec as P

VARS = 5
CHIPS_Z = 8
CHIPS_Y = 4
BLOCK = 320
FACE = 80
ELEMS = 8
RHS = 128
HANG = 32
EPS = 1e-6
GROUP = 8
VMEM_LIMIT = 40 * 1024 * 1024

TN = (((0,), (0,)), ((), ()))
NN = (((1,), (0,)), ((), ()))


def mm(a, b, dims):
    return lax.dot_general(a, b, dims, preferred_element_type=jnp.float32)


def low_half():
    return lax.broadcasted_iota(jnp.int32, (10, 8, RHS), 1) < 4


def turn(x):
    return pltpu.roll(x, 4, 1)


def trace_a(field, end):
    return field.reshape(VARS, 4, 16, RHS)[:, 3 * end].reshape(FACE, RHS)


def trace_b(field, end):
    rows = field.reshape(10, 4, 8, RHS)
    if end == 0:
        out = jnp.where(low_half(), rows[:, 0], turn(rows[:, 2]))
    else:
        out = jnp.where(low_half(), turn(rows[:, 1]), rows[:, 3])
    return out.reshape(FACE, RHS)


def spread_a(values, end):
    piece = values.reshape(VARS, 1, 16, RHS)
    zero = jnp.zeros((VARS, 3, 16, RHS), jnp.float32)
    return jnp.concatenate([zero, piece] if end else [piece, zero], axis=1).reshape(BLOCK, RHS)


def spread_b(values, end):
    rows = values.reshape(10, 8, RHS)
    zero = jnp.zeros_like(rows)
    low = low_half()
    if end == 0:
        parts = [jnp.where(low, rows, 0.0), zero, jnp.where(low, turn(rows), 0.0), zero]
    else:
        parts = [zero, jnp.where(low, 0.0, turn(rows)), zero, jnp.where(low, 0.0, rows)]
    return jnp.stack(parts, axis=1).reshape(BLOCK, RHS)


def face_c(end):
    return pl.ds(3 * end, FACE, stride=4)


def fill_traces(lowered, inv_ref, tr_ref, app_ref):
    for e in range(ELEMS):
        field = lowered(e)
        applied = mm(inv_ref[e], field, TN)
        app_ref[e] = applied
        for end in range(2):
            tr_ref[6 * e + end] = trace_a(applied, end).astype(jnp.bfloat16)
            tr_ref[6 * e + 2 + end] = trace_b(applied, end).astype(jnp.bfloat16)
            tr_ref[6 * e + 4 + end] = app_ref[e, face_c(end), :].astype(jnp.bfloat16)


def flux(face_ref, tr_ref, e, f):
    return mm(face_ref[6 * e + f], tr_ref[6 * e + f], TN)


def add_slots(acc, wanted, sign, list_ref, count_ref, hang_ref, tr_ref, slot_ref):
    live = count_ref[0, 0]

    def look(h, n):
        slot_ref[n] = h
        hit = jnp.logical_and(list_ref[2, h] * sign == wanted, h < live)
        return n + hit.astype(jnp.int32)

    n = lax.fori_loop(0, HANG, look, jnp.int32(0), unroll=8)
    for i in range(GROUP):
        slot_ref[n + i] = 0

    def work(first, size):
        parts = []
        for i in range(size):
            k = first + i
            h = slot_ref[k]
            source = list_ref[0, h] * 6 + list_ref[1, h]
            target = jnp.where(k < n, list_ref[3, h], ELEMS)
            parts.append((target, mm(hang_ref[h], tr_ref[source], TN)))
        for target, part in parts:
            acc[target] += part

    whole = (n + GROUP // 2 - 1) // GROUP

    @pl.loop(0, whole)
    def _(g):
        work(g * GROUP, GROUP)

    @pl.when(n > whole * GROUP)
    def _():
        work(whole * GROUP, GROUP // 2)


def core_and_row():
    return lax.axis_index("c"), lax.axis_index("x") % 2


def start_x(side, acc, face_ref, tr_ref):
    for n in range(4):
        acc[n + 4 * (1 - side)] = spread_a(flux(face_ref, tr_ref, n + 4 * side, side), 1 - side)
        acc[n + 4 * side] = jnp.zeros((BLOCK, RHS), jnp.float32)


def cross_part(acc, out_ref, list_ref, count_ref, face_ref, hang_ref, tr_ref, slot_ref, wanted):
    core, _ = core_and_row()
    side = core if wanted == 1 else 1 - core
    for s in range(2):

        @pl.when(side == s)
        def _(s=s):
            start_x(s, acc, face_ref, tr_ref)

    add_slots(acc, wanted, 2 * core - 1, list_ref, count_ref, hang_ref, tr_ref, slot_ref)
    out_ref[...] = acc[0:ELEMS].astype(out_ref.dtype)


def edge_fluxes(face_ref, tr_ref, ya_ref, yb_ref):
    _, odd = core_and_row()
    for parity in range(2):

        @pl.when(odd == parity)
        def _(parity=parity):
            up_ref, down_ref = (ya_ref, yb_ref) if parity == 0 else (yb_ref, ya_ref)
            for x in range(2):
                for z in range(2):
                    up_ref[2 * x + z] = flux(face_ref, tr_ref, 4 * x + 2 + z, 3)
                    down_ref[2 * x + z] = flux(face_ref, tr_ref, 4 * x + z, 2)


def first_kernel(
    list_ref, count_ref, rhs_hbm, inv_hbm, face_hbm, hang_hbm,
    rhs_ref, inv_ref, face_ref, hang_ref, tr_ref, cross_ref, acc, app_ref, slot_ref, sems,
):
    copies = []

    def bring(source, target):
        copies.append(pltpu.make_async_copy(source, target, sems.at[len(copies)]))
        copies[-1].start()

    for e in range(0, ELEMS, 2):
        pair = pl.ds(e, 2)
        bring(rhs_hbm.at[pair], rhs_ref.at[pair])
        bring(inv_hbm.at[pair], inv_ref.at[pair])
    late = len(copies)
    bring(face_hbm, face_ref)
    for h in range(0, HANG, 8):
        bring(hang_hbm.at[pl.ds(h, 8)], hang_ref.at[pl.ds(h, 8)])

    def lowered(e):
        if e % 2 == 0:
            copies[e].wait()
            copies[e + 1].wait()
        return rhs_ref[e]

    fill_traces(lowered, inv_ref, tr_ref, app_ref)
    for copy in copies[late:]:
        copy.wait()
    cross_part(acc, cross_ref, list_ref, count_ref, face_ref, hang_ref, tr_ref, slot_ref, 1)


def side_kernel(list_ref, count_ref, face_ref, hang_ref, tr_ref, chip_ref, ya_ref, yb_ref, acc, slot_ref):
    edge_fluxes(face_ref, tr_ref, ya_ref, yb_ref)
    cross_part(acc, chip_ref, list_ref, count_ref, face_ref, hang_ref, tr_ref, slot_ref, -1)


def own_body(list_ref, count_ref, face_ref, hang_ref, tr_ref, own_ref, acc, slot_ref):
    for e in range(ELEMS):
        x, y, z = (e >> 2) & 1, (e >> 1) & 1, e & 1
        from_x = flux(face_ref, tr_ref, e ^ 4, 0 if x == 0 else 1)
        from_y = flux(face_ref, tr_ref, e ^ 2, 2 if y == 0 else 3)
        from_z = flux(face_ref, tr_ref, e ^ 1, 4 if z == 0 else 5)
        acc[e] = spread_a(from_x, 1 - x) + spread_b(from_y, 1 - y)
        acc[e, face_c(1 - z), :] += from_z
    add_slots(acc, 0, 1, list_ref, count_ref, hang_ref, tr_ref, slot_ref)
    own_ref[...] = acc[0:ELEMS]


def own_kernel(list_ref, count_ref, face_ref, hang_ref, tr_ref, own_ref, acc, slot_ref):
    own_body(list_ref, count_ref, face_ref, hang_ref, tr_ref, own_ref, acc, slot_ref)


def inner(e, *pairs):
    return [jnp.sum((a[e].astype(jnp.float32) * b[e].astype(jnp.float32)).reshape(BLOCK // 8, 8, RHS), axis=0) for a, b in pairs]


def gram_rows(*pairs):
    totals = inner(0, *pairs)
    for e in range(1, ELEMS):
        totals = [t + p for t, p in zip(totals, inner(e, *pairs))]
    rows = [jnp.sum(t, axis=0, keepdims=True) for t in totals]
    return jnp.concatenate(rows, axis=1)


def own_gram_kernel(
    list_ref, count_ref, face_ref, hang_ref, tr_ref, rhs_ref, w1_ref, own_ref, gram_ref, acc, slot_ref
):
    own_body(list_ref, count_ref, face_ref, hang_ref, tr_ref, own_ref, acc, slot_ref)
    gram_ref[...] = gram_rows((rhs_ref, rhs_ref), (rhs_ref, w1_ref), (w1_ref, w1_ref))


def land(w_ref, own_ref, cross_ref, chip_ref, ya_ref, yb_ref):
    _, odd = core_and_row()
    for parity in range(2):

        @pl.when(odd == parity)
        def _(parity=parity):
            from_up, from_down = (ya_ref, yb_ref) if parity == 0 else (yb_ref, ya_ref)
            for e in range(ELEMS):
                y = (e >> 1) & 1
                n = 2 * (e >> 2) + (e & 1)
                edge = spread_b(from_up[n], 1) if y else spread_b(from_down[n], 0)
                came = cross_ref[e].astype(jnp.float32) + chip_ref[e].astype(jnp.float32)
                w_ref[e] = own_ref[e] + came + edge


def second_kernel(
    list_ref, count_ref, own_ref, in_cross, in_chip, in_ya, in_yb, inv_ref, face_ref, hang_ref,
    w_ref, tr_ref, cross_ref, acc, app_ref, slot_ref,
):
    land(w_ref, own_ref, in_cross, in_chip, in_ya, in_yb)
    fill_traces(lambda e: w_ref[e].astype(jnp.bfloat16), inv_ref, tr_ref, app_ref)
    cross_part(acc, cross_ref, list_ref, count_ref, face_ref, hang_ref, tr_ref, slot_ref, 1)


def last_kernel(own_ref, in_cross, in_chip, in_ya, in_yb, rhs_ref, w1_ref, early_ref, w_ref, keep_ref, give_ref):
    land(w_ref, own_ref, in_cross, in_chip, in_ya, in_yb)
    late = gram_rows((rhs_ref, w_ref), (w1_ref, w_ref), (w_ref, w_ref))
    early = early_ref[...]
    core, _ = core_and_row()
    keep_ref[...] = jnp.where(core == 0, early, late)
    give_ref[...] = jnp.where(core == 0, late, early)


def combine_kernel(entries, mine_ref, other_ref, rhs_ref, w1_ref, w2_ref, out_hbm, hess_ref, out_ref, sems):
    core, _ = core_and_row()
    mine = mine_ref[...] * (1.0 / entries)
    other = other_ref[...] * (1.0 / entries)
    early = jnp.where(core == 0, mine, other)
    late = jnp.where(core == 0, other, mine)
    g00, g01, g11 = (early[:, RHS * i : RHS * i + RHS] for i in range(3))
    g02, g12, g22 = (late[:, RHS * i : RHS * i + RHS] for i in range(3))
    norm0 = g00 + EPS
    size0 = jnp.sqrt(norm0)
    h11 = (g00 + g01) / norm0
    c1 = (EPS - g01) / norm0
    square1 = jnp.maximum(g11 + 2.0 * c1 * g01 + c1 * c1 * g00, 0.0) / norm0 + EPS
    h21 = jnp.sqrt(square1)
    s2 = 1.0 / (size0 * h21)
    ratio = (g02 + c1 * g01 + EPS * h11) / norm0
    h12 = ratio * s2 * size0
    q = EPS / square1 - s2 * s2 * (g12 + c1 * (g11 + g02 + c1 * g01))
    h22 = 1.0 - q
    alpha = c1 + q
    beta = c1 * q - ratio
    total = g22 + 2.0 * (alpha * g12 + beta * g02 + alpha * beta * g01)
    total = total + alpha * alpha * g11 + beta * beta * g00
    h32 = jnp.sqrt(s2 * s2 * jnp.maximum(total, 0.0) + EPS)
    zero = jnp.zeros_like(h11)
    for i, row in enumerate(((h11, h12), (h21, h22), (zero, h32))):
        hess_ref[i] = jnp.concatenate(row, axis=0)
    k2 = s2 / h32
    k1 = k2 * alpha
    k0 = k2 * beta
    copies = []
    for e in range(ELEMS):
        out_ref[e] = k2 * w2_ref[e] + k1 * w1_ref[e] + k0 * rhs_ref[e].astype(jnp.float32)
        copies.append(pltpu.make_async_copy(out_ref.at[e], out_hbm.at[e], sems.at[e]))
        copies[e].start()
    for copy in copies:
        copy.wait()


def shape(dims, dtype=jnp.float32):
    return jax.ShapeDtypeStruct(dims, dtype)


FIELD = (ELEMS, BLOCK, RHS)
TRACES = (6 * ELEMS, FACE, RHS)
SIDE = (4, FACE, RHS)
SMEM = pl.BlockSpec(memory_space=pltpu.SMEM)
VMEM = pl.BlockSpec(memory_space=pltpu.VMEM)
HBM = pl.BlockSpec(memory_space=pltpu.HBM)


def call(kernel, in_specs, outs, scratch, flops, moved, out_specs=None):
    return pl.pallas_call(
        kernel,
        out_shape=outs,
        in_specs=in_specs,
        out_specs=out_specs or [VMEM] * len(outs),
        scratch_shapes=scratch,
        compiler_params=pltpu.CompilerParams(vmem_limit_bytes=VMEM_LIMIT),
        cost_estimate=pl.CostEstimate(flops=flops, bytes_accessed=moved, transcendentals=0),
    )


def stay(x):
    return pltpu.with_memory_space_constraint(x, pltpu.HBM)


def per_device(entries, pairs, rhs_field, inv_block, face_block, hang_list, hang_count, hang_block):
    rows = stay(hang_list.reshape(HANG, 4).T)
    count = hang_count
    field = pltpu.VMEM(FIELD, jnp.float32)
    acc = pltpu.VMEM((ELEMS + 1, BLOCK, RHS), jnp.float32)
    slots = pltpu.SMEM((HANG + 8,), jnp.int32)
    bf16 = jnp.bfloat16
    million = 10**6
    scalars = [SMEM, SMEM]

    rhs, inv, face, hang, traces, cross = call(
        first_kernel, scalars + [HBM] * 4,
        [
            shape(FIELD, bf16), shape((ELEMS, BLOCK, BLOCK), bf16), shape((6 * ELEMS, FACE, FACE), bf16),
            shape((HANG, FACE, BLOCK), bf16), shape(TRACES, bf16), shape(FIELD, bf16),
        ],
        [acc, field, slots, pltpu.SemaphoreType.DMA((ELEMS + 5,))],
        300 * million, 6 * million,
    )(
        rows, count, stay(rhs_field.reshape(FIELD)), stay(inv_block.reshape(ELEMS, BLOCK, BLOCK)),
        stay(face_block.reshape(6 * ELEMS, FACE, FACE)), stay(hang_block.reshape(HANG, FACE, BLOCK)),
    )

    def exchange(traces, cross, own_call):
        in_cross = lax.ppermute(cross, ("z", "y", "c"), pairs["cross"])
        chip, ya, yb = call(
            side_kernel, scalars + [VMEM] * 3, [shape(FIELD, bf16), shape(SIDE), shape(SIDE)], [acc, slots],
            100 * million, 4 * million,
        )(rows, count, face, hang, traces)
        in_ya = lax.ppermute(ya, "x", pairs["even"])
        in_yb = lax.ppermute(yb, "x", pairs["odd"])
        in_chip = lax.ppermute(chip, "c", [(0, 1), (1, 0)])
        return own_call(traces), (in_cross, in_chip, in_ya, in_yb)

    def own_first(traces):
        return call(
            own_kernel, scalars + [VMEM] * 3, [shape(FIELD)], [acc, slots], 100 * million, 6 * million
        )(rows, count, face, hang, traces)[0]

    own, arrived = exchange(traces, cross, own_first)
    w1, traces, cross = call(
        second_kernel, scalars + [VMEM] * 8, [shape(FIELD), shape(TRACES, bf16), shape(FIELD, bf16)],
        [acc, field, slots], 300 * million, 8 * million,
    )(rows, count, own, *arrived, inv, face, hang)

    def own_second(traces):
        return call(
            own_gram_kernel, scalars + [VMEM] * 5, [shape(FIELD), shape((1, 3 * RHS))], [acc, slots],
            100 * million, 6 * million,
        )(rows, count, face, hang, traces, rhs, w1)

    (own, early), arrived = exchange(traces, cross, own_second)
    w2, keep, give = call(
        last_kernel, [VMEM] * 8, [shape(FIELD), shape((1, 3 * RHS)), shape((1, 3 * RHS))], [], 10 * million, 8 * million
    )(own, *arrived, rhs, w1, early)

    swap = [(0, 1), (1, 0)]
    part = keep + lax.ppermute(give, "c", swap)
    chips = lax.axis_size(("z", "y", "x"))
    mine = lax.all_to_all(jnp.broadcast_to(part, (chips, 1, 3 * RHS)), ("z", "y", "x"), 0, 0).sum(0)
    last, hessenberg = call(
        functools.partial(combine_kernel, entries), [VMEM] * 5, [shape(FIELD), shape((3, 2, RHS))],
        [field, pltpu.SemaphoreType.DMA((ELEMS,))], 10 * million, 6 * million, [HBM, VMEM],
    )(mine, lax.ppermute(mine, "c", swap), rhs, w1, w2)
    return last.reshape(rhs_field.shape), hessenberg


def solution(mesh):
    count_x, count_y = mesh.shape["gx"], mesh.shape["gy"]
    grid = jax.sharding.Mesh(
        mesh.devices.reshape(CHIPS_Z, CHIPS_Y, 2, count_y), ("z", "y", "c", "x")
    )
    pairs = {"cross": [], "even": [], "odd": []}
    for i in range(1, count_x - 1, 2):
        pairs["cross"] += [(i, i + 1), (i + 1, i)]
    for j in range(count_y - 1):
        pairs["odd" if j % 2 else "even"] += [(j, j + 1), (j + 1, j)]
    long = ("z", "y", "c")
    in_specs = (P(long, "x"),) * 6
    out_specs = (P(long, "x"), P())
    entries = float(ELEMS * BLOCK * count_x * count_y)
    return jax.shard_map(
        functools.partial(per_device, entries, pairs),
        mesh=grid, in_specs=in_specs, out_specs=out_specs, check_vma=False,
    )
```

```python
import functools

import jax
import jax.numpy as jnp
from jax import lax
from jax.experimental import pallas as pl
from jax.experimental.pallas import tpu as pltpu
from jax.sharding import PartitionSpec as P

VARS = 5
CHIPS_Z = 8
CHIPS_Y = 4
BLOCK = 320
FACE = 80
ELEMS = 8
RHS = 128
HANG = 32
EPS = 1e-6
GROUP = 8
SIDE_FLOPS = 100 * 10**6
OWN_FLOPS = 4000 * 10**6
VMEM_LIMIT = 40 * 1024 * 1024

TN = (((0,), (0,)), ((), ()))
NN = (((1,), (0,)), ((), ()))


def mm(a, b, dims):
    return lax.dot_general(a, b, dims, preferred_element_type=jnp.float32)


def low_half():
    return lax.broadcasted_iota(jnp.int32, (10, 8, RHS), 1) < 4


def turn(x):
    return pltpu.roll(x, 4, 1)


def trace_a(field, end):
    return field.reshape(VARS, 4, 16, RHS)[:, 3 * end].reshape(FACE, RHS)


def trace_b(field, end):
    rows = field.reshape(10, 4, 8, RHS)
    if end == 0:
        out = jnp.where(low_half(), rows[:, 0], turn(rows[:, 2]))
    else:
        out = jnp.where(low_half(), turn(rows[:, 1]), rows[:, 3])
    return out.reshape(FACE, RHS)


def spread_a(values, end):
    piece = values.reshape(VARS, 1, 16, RHS)
    zero = jnp.zeros((VARS, 3, 16, RHS), jnp.float32)
    return jnp.concatenate([zero, piece] if end else [piece, zero], axis=1).reshape(BLOCK, RHS)


def spread_b(values, end):
    rows = values.reshape(10, 8, RHS)
    zero = jnp.zeros_like(rows)
    low = low_half()
    if end == 0:
        parts = [jnp.where(low, rows, 0.0), zero, jnp.where(low, turn(rows), 0.0), zero]
    else:
        parts = [zero, jnp.where(low, 0.0, turn(rows)), zero, jnp.where(low, 0.0, rows)]
    return jnp.stack(parts, axis=1).reshape(BLOCK, RHS)


def face_c(end):
    return pl.ds(3 * end, FACE, stride=4)


def fill_traces(lowered, inv_ref, tr_ref, app_ref):
    for e in range(ELEMS):
        field = lowered(e)
        applied = mm(inv_ref[e], field, TN)
        app_ref[e] = applied
        for end in range(2):
            tr_ref[6 * e + end] = trace_a(applied, end).astype(jnp.bfloat16)
            tr_ref[6 * e + 2 + end] = trace_b(applied, end).astype(jnp.bfloat16)
            tr_ref[6 * e + 4 + end] = app_ref[e, face_c(end), :].astype(jnp.bfloat16)


def list_slots(wanted, sign, list_ref, count_ref, slot_ref):
    live = count_ref[0, 0]

    def look(h, n):
        slot_ref[n] = h
        hit = jnp.logical_and(list_ref[2, h] * sign == wanted, h < live)
        return n + hit.astype(jnp.int32)

    n = lax.fori_loop(0, HANG, look, jnp.int32(0), unroll=8)
    for i in range(GROUP):
        slot_ref[n + i] = 0
    return n


def each_slot(n, slot_ref, hang_hbm, hang_ref, sems, act):
    @pl.loop(0, n)
    def _(k):
        act(pltpu.make_async_copy(hang_hbm.at[slot_ref[k]], hang_ref.at[k], sems.at[k]))


def add_slots(acc, n, list_ref, hang_ref, tr_ref, slot_ref):
    def work(first, size):
        parts = []
        for i in range(size):
            k = first + i
            h = slot_ref[k]
            source = list_ref[0, h] * 6 + list_ref[1, h]
            target = jnp.where(k < n, list_ref[3, h], ELEMS)
            parts.append((target, mm(hang_ref[k], tr_ref[source], TN)))
        for target, part in parts:
            acc[target] += part

    whole = (n + GROUP // 2 - 1) // GROUP

    @pl.loop(0, whole)
    def _(g):
        work(g * GROUP, GROUP)

    @pl.when(n > whole * GROUP)
    def _():
        work(whole * GROUP, GROUP // 2)


def core_and_row():
    return lax.axis_index("c"), lax.axis_index("x") % 2


def flux(weights, tr_ref, e, f):
    return mm(weights, tr_ref[6 * e + f], TN)


def swap_if(flag, a, b):
    return jnp.where(flag, b, a), jnp.where(flag, a, b)


def edge_fluxes(face_ref, tr_ref, ya_ref, yb_ref):
    _, odd = core_and_row()
    for x in range(2):
        for z in range(2):
            up = flux(face_ref[1, x, z], tr_ref, 4 * x + 2 + z, 3)
            down = flux(face_ref[2, x, z], tr_ref, 4 * x + z, 2)
            first, second = swap_if(odd == 1, up, down)
            ya_ref[2 * x + z] = first.astype(jnp.bfloat16)
            yb_ref[2 * x + z] = second.astype(jnp.bfloat16)


def cross_part(acc, out_refs, n, side, list_ref, face_ref, hang_ref, tr_ref, slot_ref):
    for m in range(4):
        piece = flux(face_ref[0, m // 2, m % 2], tr_ref, m + 4 * side, side)
        acc[m + 4 * (1 - side)] = jnp.where(side == 1, spread_a(piece, 0), spread_a(piece, 1))
        acc[m + 4 * side] = jnp.zeros((BLOCK, RHS), jnp.float32)
    add_slots(acc, n, list_ref, hang_ref, tr_ref, slot_ref)
    for i, ref in enumerate(out_refs):
        size = ref.shape[0]
        ref[...] = acc[size * i : size * i + size].astype(ref.dtype)


def first_kernel(
    list_hbm, count_ref, rhs_hbm, inv_hbm, face_hbm, hang_hbm,
    rhs_ref, inv_ref, face_ref, hang_ref, tr_ref, cross_ref, ya_ref, yb_ref,
    acc, app_ref, list_ref, slot_ref, sems, hang_sems,
):
    core, _ = core_and_row()
    copies = []

    def bring(source, target):
        copies.append(pltpu.make_async_copy(source, target, sems.at[len(copies)]))
        copies[-1].start()

    bring(list_hbm, list_ref)
    for e in range(0, ELEMS, 2):
        pair = pl.ds(e, 2)
        bring(rhs_hbm.at[pair], rhs_ref.at[pair])
        bring(inv_hbm.at[pair], inv_ref.at[pair])
    late = len(copies)
    bring(face_hbm.at[core, :, :, core], face_ref.at[0])
    bring(face_hbm.at[:, 1, :, 3], face_ref.at[1])
    bring(face_hbm.at[:, 0, :, 2], face_ref.at[2])
    copies[0].wait()
    n = list_slots(1, 2 * core - 1, list_ref, count_ref, slot_ref)
    each_slot(n, slot_ref, hang_hbm, hang_ref, hang_sems, lambda copy: copy.start())

    def lowered(e):
        if e % 2 == 0:
            copies[e + 1].wait()
            copies[e + 2].wait()
        return rhs_ref[e]

    fill_traces(lowered, inv_ref, tr_ref, app_ref)
    for copy in copies[late:]:
        copy.wait()
    edge_fluxes(face_ref, tr_ref, ya_ref, yb_ref)
    each_slot(n, slot_ref, hang_hbm, hang_ref, hang_sems, lambda copy: copy.wait())
    cross_part(acc, (cross_ref,), n, core, list_ref, face_ref, hang_ref, tr_ref, slot_ref)


def side_first_kernel(
    list_ref, count_ref, face_hbm, hang_hbm, tr_ref, chip_ref, chip2_ref, face_ref, hang_ref, own_face_ref, own_hang_ref,
    acc, slot_ref, own_slot_ref, sems, hang_sems, own_hang_sems,
):
    core, _ = core_and_row()
    pieces = [
        face_hbm.at[1, :, :, 0], face_hbm.at[0, :, :, 1], face_hbm.at[:, 1, :, 2],
        face_hbm.at[:, 0, :, 3], face_hbm.at[:, :, 1, 4], face_hbm.at[:, :, 0, 5],
    ]
    copies = [pltpu.make_async_copy(face_hbm.at[1 - core, :, :, 1 - core], face_ref.at[0], sems.at[6])]
    copies += [pltpu.make_async_copy(p, own_face_ref.at[f], sems.at[f]) for f, p in enumerate(pieces)]
    copies[0].start()
    n = list_slots(-1, 2 * core - 1, list_ref, count_ref, slot_ref)
    each_slot(n, slot_ref, hang_hbm, hang_ref, hang_sems, lambda copy: copy.start())
    for copy in copies[1:]:
        copy.start()
    own_n = list_slots(0, 1, list_ref, count_ref, own_slot_ref)
    each_slot(own_n, own_slot_ref, hang_hbm, own_hang_ref, own_hang_sems, lambda copy: copy.start())
    copies[0].wait()
    each_slot(n, slot_ref, hang_hbm, hang_ref, hang_sems, lambda copy: copy.wait())
    cross_part(acc, (chip_ref, chip2_ref), n, 1 - core, list_ref, face_ref, hang_ref, tr_ref, slot_ref)
    for copy in copies[1:]:
        copy.wait()
    each_slot(own_n, own_slot_ref, hang_hbm, own_hang_ref, own_hang_sems, lambda copy: copy.wait())


def side_second_kernel(list_ref, count_ref, face_ref, hang_ref, tr_ref, chip_ref, chip2_ref, acc, slot_ref):
    core, _ = core_and_row()
    n = list_slots(-1, 2 * core - 1, list_ref, count_ref, slot_ref)
    cross_part(acc, (chip_ref, chip2_ref), n, 1 - core, list_ref, face_ref, hang_ref, tr_ref, slot_ref)


def own_part(n, list_ref, face_ref, hang_ref, tr_ref, own_ref, acc, slot_ref):
    for e in range(ELEMS):
        x, y, z = (e >> 2) & 1, (e >> 1) & 1, e & 1
        from_x = flux(face_ref[x, y, z], tr_ref, e ^ 4, x)
        from_y = flux(face_ref[2 + y, x, z], tr_ref, e ^ 2, 2 + y)
        from_z = flux(face_ref[4 + z, x, y], tr_ref, e ^ 1, 4 + z)
        acc[e] = spread_a(from_x, 1 - x) + spread_b(from_y, 1 - y)
        acc[e, face_c(1 - z), :] += from_z
    add_slots(acc, n, list_ref, hang_ref, tr_ref, slot_ref)
    own_ref[...] = acc[0:ELEMS]


def own_kernel(list_ref, count_ref, face_ref, hang_ref, tr_ref, own_ref, acc, slot_ref):
    n = list_slots(0, 1, list_ref, count_ref, slot_ref)
    own_part(n, list_ref, face_ref, hang_ref, tr_ref, own_ref, acc, slot_ref)


def inner(e, *pairs):
    return [jnp.sum((a[e].astype(jnp.float32) * b[e].astype(jnp.float32)).reshape(BLOCK // 8, 8, RHS), axis=0) for a, b in pairs]


def gram_rows(*pairs):
    totals = inner(0, *pairs)
    for e in range(1, ELEMS):
        totals = [t + p for t, p in zip(totals, inner(e, *pairs))]
    rows = [jnp.sum(t, axis=0, keepdims=True) for t in totals]
    return jnp.concatenate(rows, axis=1)


def own_gram_kernel(
    list_ref, count_ref, face_ref, hang_ref, tr_ref, rhs_ref, w1_ref, own_ref, gram_ref, acc, slot_ref
):
    n = list_slots(0, 1, list_ref, count_ref, slot_ref)
    own_part(n, list_ref, face_ref, hang_ref, tr_ref, own_ref, acc, slot_ref)
    gram_ref[...] = gram_rows((rhs_ref, rhs_ref), (rhs_ref, w1_ref), (w1_ref, w1_ref))


def landed(e, own_ref, cross_ref, chip_refs, ya_ref, yb_ref):
    _, odd = core_and_row()
    y = (e >> 1) & 1
    n = 2 * (e >> 2) + (e & 1)
    edge = swap_if(odd == 1, ya_ref[n].astype(jnp.float32), yb_ref[n].astype(jnp.float32))[1 - y]
    came = cross_ref[e].astype(jnp.float32) + chip_refs[e // 4][e % 4].astype(jnp.float32)
    return own_ref[e] + came + spread_b(edge, y)


def second_kernel(
    list_ref, count_ref, own_ref, in_cross, in_chip, in_chip2, in_ya, in_yb, inv_ref, face_ref, hang_ref,
    w_ref, tr_ref, cross_ref, ya_ref, yb_ref, acc, app_ref, slot_ref,
):

    def lowered(e):
        w = landed(e, own_ref, in_cross, (in_chip, in_chip2), in_ya, in_yb)
        w_ref[e] = w
        return w.astype(jnp.bfloat16)

    fill_traces(lowered, inv_ref, tr_ref, app_ref)
    edge_fluxes(face_ref, tr_ref, ya_ref, yb_ref)
    core, _ = core_and_row()
    n = list_slots(1, 2 * core - 1, list_ref, count_ref, slot_ref)
    cross_part(acc, (cross_ref,), n, core, list_ref, face_ref, hang_ref, tr_ref, slot_ref)


def last_kernel(own_ref, in_cross, in_chip, in_chip2, in_ya, in_yb, rhs_ref, w1_ref, early_ref, w_ref, keep_ref, give_ref):
    for e in range(ELEMS):
        w_ref[e] = landed(e, own_ref, in_cross, (in_chip, in_chip2), in_ya, in_yb)
    late = gram_rows((rhs_ref, w_ref), (w1_ref, w_ref), (w_ref, w_ref))
    early = early_ref[...]
    core, _ = core_and_row()
    keep_ref[...] = jnp.where(core == 0, early, late)
    give_ref[...] = jnp.where(core == 0, late, early)


def combine_kernel(entries, mine_ref, other_ref, rhs_ref, w1_ref, w2_ref, out_hbm, hess_ref, out_ref, sems):
    core, _ = core_and_row()
    mine = mine_ref[...] * (1.0 / entries)
    other = other_ref[...] * (1.0 / entries)
    early = jnp.where(core == 0, mine, other)
    late = jnp.where(core == 0, other, mine)
    g00, g01, g11 = (early[:, RHS * i : RHS * i + RHS] for i in range(3))
    g02, g12, g22 = (late[:, RHS * i : RHS * i + RHS] for i in range(3))
    norm0 = g00 + EPS
    size0 = jnp.sqrt(norm0)
    h11 = (g00 + g01) / norm0
    c1 = (EPS - g01) / norm0
    square1 = jnp.maximum(g11 + 2.0 * c1 * g01 + c1 * c1 * g00, 0.0) / norm0 + EPS
    h21 = jnp.sqrt(square1)
    s2 = 1.0 / (size0 * h21)
    ratio = (g02 + c1 * g01 + EPS * h11) / norm0
    h12 = ratio * s2 * size0
    q = EPS / square1 - s2 * s2 * (g12 + c1 * (g11 + g02 + c1 * g01))
    h22 = 1.0 - q
    alpha = c1 + q
    beta = c1 * q - ratio
    total = g22 + 2.0 * (alpha * g12 + beta * g02 + alpha * beta * g01)
    total = total + alpha * alpha * g11 + beta * beta * g00
    h32 = jnp.sqrt(s2 * s2 * jnp.maximum(total, 0.0) + EPS)
    zero = jnp.zeros_like(h11)
    for i, row in enumerate(((h11, h12), (h21, h22), (zero, h32))):
        hess_ref[i] = jnp.concatenate(row, axis=0)
    k2 = s2 / h32
    k1 = k2 * alpha
    k0 = k2 * beta
    copies = []
    for e in range(ELEMS):
        out_ref[e] = k2 * w2_ref[e] + k1 * w1_ref[e] + k0 * rhs_ref[e].astype(jnp.float32)
        copies.append(pltpu.make_async_copy(out_ref.at[e], out_hbm.at[e], sems.at[e]))
        copies[e].start()
    for copy in copies:
        copy.wait()


def shape(dims, dtype=jnp.float32):
    return jax.ShapeDtypeStruct(dims, dtype)


FIELD = (ELEMS, BLOCK, RHS)
TRACES = (6 * ELEMS, FACE, RHS)
SIDE = (4, FACE, RHS)
HALF = (4, BLOCK, RHS)
SMEM = pl.BlockSpec(memory_space=pltpu.SMEM)
VMEM = pl.BlockSpec(memory_space=pltpu.VMEM)
HBM = pl.BlockSpec(memory_space=pltpu.HBM)


def call(kernel, in_specs, outs, scratch, flops, moved, out_specs=None):
    return pl.pallas_call(
        kernel,
        out_shape=outs,
        in_specs=in_specs,
        out_specs=out_specs or [VMEM] * len(outs),
        scratch_shapes=scratch,
        compiler_params=pltpu.CompilerParams(vmem_limit_bytes=VMEM_LIMIT),
        cost_estimate=pl.CostEstimate(flops=flops, bytes_accessed=moved, transcendentals=0),
    )


def stay(x):
    return pltpu.with_memory_space_constraint(x, pltpu.HBM)


def per_device(entries, pairs, rhs_field, inv_block, face_block, hang_list, hang_count, hang_block):
    rows = stay(hang_list.reshape(HANG, 4).T)
    count = hang_count
    field = pltpu.VMEM(FIELD, jnp.float32)
    acc = pltpu.VMEM((ELEMS + 1, BLOCK, RHS), jnp.float32)
    slots = pltpu.SMEM((HANG + 8,), jnp.int32)
    bf16 = jnp.bfloat16
    million = 10**6
    scalars = [SMEM, SMEM]
    sems = lambda n: pltpu.SemaphoreType.DMA((n,))
    faces = stay(face_block)
    hangs = stay(hang_block.reshape(HANG, FACE, BLOCK))
    packed = shape((HANG, FACE, BLOCK), bf16)
    held = lambda n: shape((n, 2, 2, FACE, FACE), bf16)
    halves = [shape(HALF, bf16)] * 2
    sent = [shape(TRACES, bf16), shape(FIELD, bf16), shape(SIDE, bf16), shape(SIDE, bf16)]

    rhs, inv, face, hang, traces, *out = call(
        first_kernel, [HBM, SMEM] + [HBM] * 4, [shape(FIELD, bf16), shape((ELEMS, BLOCK, BLOCK), bf16), held(3), packed] + sent,
        [
            acc, field, pltpu.SMEM((4, HANG), jnp.int32), slots,
            sems(ELEMS + 4), sems(HANG),
        ],
        300 * million, 6 * million,
    )(rows, count, stay(rhs_field.reshape(FIELD)), stay(inv_block.reshape(ELEMS, BLOCK, BLOCK)), faces, hangs)

    def exchange(out, side_call, own_call):
        cross, ya, yb = out
        in_cross = lax.ppermute(cross, ("z", "y", "c"), pairs["cross"])
        in_ya = lax.ppermute(ya, "x", pairs["even"])
        in_yb = lax.ppermute(yb, "x", pairs["odd"])
        low, high, *weights = side_call()
        in_chip = [lax.ppermute(part, "c", [(0, 1), (1, 0)]) for part in (low, high)]
        own, *rest = own_call(weights[2:])
        return (own, in_cross, *in_chip, in_ya, in_yb), weights, rest

    def side_first():
        return call(
            side_first_kernel, scalars + [HBM, HBM, VMEM], halves + [held(1), packed, held(6), packed],
            [acc, slots, slots, sems(7), sems(HANG), sems(HANG)], SIDE_FLOPS, 4 * million,
        )(rows, count, faces, hangs, traces)

    def own_first(weights):
        return call(own_kernel, scalars + [VMEM] * 3, [shape(FIELD)], [acc, slots], OWN_FLOPS, 6 * million)(
            rows, count, *weights, traces
        )

    arrived, weights, _ = exchange(out, side_first, own_first)
    w1, traces, *out = call(
        second_kernel, scalars + [VMEM] * 9, [shape(FIELD)] + sent, [acc, field, slots], 300 * million, 8 * million,
    )(rows, count, *arrived, inv, face, hang)

    def side_second():
        return call(side_second_kernel, scalars + [VMEM] * 3, halves, [acc, slots], SIDE_FLOPS, 4 * million)(
            rows, count, *weights[:2], traces
        )

    def own_second(_):
        return call(
            own_gram_kernel, scalars + [VMEM] * 5, [shape(FIELD), shape((1, 3 * RHS))], [acc, slots],
            OWN_FLOPS, 6 * million,
        )(rows, count, *weights[2:], traces, rhs, w1)

    arrived, _, (early,) = exchange(out, side_second, own_second)
    w2, keep, give = call(
        last_kernel, [VMEM] * 9, [shape(FIELD), shape((1, 3 * RHS)), shape((1, 3 * RHS))], [], 10 * million, 8 * million
    )(*arrived, rhs, w1, early)

    swap = [(0, 1), (1, 0)]
    part = keep + lax.ppermute(give, "c", swap)
    chips = lax.axis_size(("z", "y", "x"))
    mine = lax.all_to_all(jnp.broadcast_to(part, (chips, 1, 3 * RHS)), ("z", "y", "x"), 0, 0).sum(0)
    last, hessenberg = call(
        functools.partial(combine_kernel, entries), [VMEM] * 5, [shape(FIELD), shape((3, 2, RHS))],
        [field, pltpu.SemaphoreType.DMA((ELEMS,))], 10 * million, 6 * million, [HBM, VMEM],
    )(mine, lax.ppermute(mine, "c", swap), rhs, w1, w2)
    return last.reshape(rhs_field.shape), hessenberg


def solution(mesh):
    count_x, count_y = mesh.shape["gx"], mesh.shape["gy"]
    grid = jax.sharding.Mesh(
        mesh.devices.reshape(CHIPS_Z, CHIPS_Y, 2, count_y), ("z", "y", "c", "x")
    )
    pairs = {"cross": [], "even": [], "odd": []}
    for i in range(1, count_x - 1, 2):
        pairs["cross"] += [(i, i + 1), (i + 1, i)]
    for j in range(count_y - 1):
        pairs["odd" if j % 2 else "even"] += [(j, j + 1), (j + 1, j)]
    long = ("z", "y", "c")
    in_specs = (P(long, "x"),) * 6
    out_specs = (P(long, "x"), P())
    entries = float(ELEMS * BLOCK * count_x * count_y)
    return jax.shard_map(
        functools.partial(per_device, entries, pairs),
        mesh=grid, in_specs=in_specs, out_specs=out_specs, check_vma=False,
    )
```

```python
import functools

import jax
import jax.numpy as jnp
from jax import lax
from jax.experimental import pallas as pl
from jax.experimental.pallas import tpu as pltpu
from jax.sharding import PartitionSpec as P

VARS = 5
CHIPS_Z = 8
CHIPS_Y = 4
BLOCK = 320
FACE = 80
ELEMS = 8
RHS = 128
HANG = 32
EPS = 1e-6
GROUP = 8
SIDE_FLOPS = 100 * 10**6
OWN_FLOPS = 4000 * 10**6
VMEM_LIMIT = 40 * 1024 * 1024

TN = (((0,), (0,)), ((), ()))
NN = (((1,), (0,)), ((), ()))


def mm(a, b, dims):
    return lax.dot_general(a, b, dims, preferred_element_type=jnp.float32)


def low_half():
    return lax.broadcasted_iota(jnp.int32, (10, 8, RHS), 1) < 4


def turn(x):
    return pltpu.roll(x, 4, 1)


def trace_a(field, end):
    return field.reshape(VARS, 4, 16, RHS)[:, 3 * end].reshape(FACE, RHS)


def trace_b(field, end):
    rows = field.reshape(10, 4, 8, RHS)
    if end == 0:
        out = jnp.where(low_half(), rows[:, 0], turn(rows[:, 2]))
    else:
        out = jnp.where(low_half(), turn(rows[:, 1]), rows[:, 3])
    return out.reshape(FACE, RHS)


def spread_a(values, end):
    piece = values.reshape(VARS, 1, 16, RHS)
    zero = jnp.zeros((VARS, 3, 16, RHS), jnp.float32)
    return jnp.concatenate([zero, piece] if end else [piece, zero], axis=1).reshape(BLOCK, RHS)


def spread_b(values, end):
    rows = values.reshape(10, 8, RHS)
    zero = jnp.zeros_like(rows)
    low = low_half()
    if end == 0:
        parts = [jnp.where(low, rows, 0.0), zero, jnp.where(low, turn(rows), 0.0), zero]
    else:
        parts = [zero, jnp.where(low, 0.0, turn(rows)), zero, jnp.where(low, 0.0, rows)]
    return jnp.stack(parts, axis=1).reshape(BLOCK, RHS)


def face_c(end):
    return pl.ds(3 * end, FACE, stride=4)


def fill_traces(lowered, inv_ref, tr_ref, app_ref):
    for e in range(ELEMS):
        field = lowered(e)
        applied = mm(inv_ref[e], field, TN)
        app_ref[e] = applied
        for end in range(2):
            tr_ref[6 * e + end] = trace_a(applied, end).astype(jnp.bfloat16)
            tr_ref[6 * e + 2 + end] = trace_b(applied, end).astype(jnp.bfloat16)
            tr_ref[6 * e + 4 + end] = app_ref[e, face_c(end), :].astype(jnp.bfloat16)


def list_slots(wanted, sign, list_ref, count_ref, slot_ref):
    live = count_ref[0, 0]

    def look(h, n):
        slot_ref[n] = h
        hit = jnp.logical_and(list_ref[2, h] * sign == wanted, h < live)
        return n + hit.astype(jnp.int32)

    n = lax.fori_loop(0, HANG, look, jnp.int32(0), unroll=8)
    for i in range(GROUP):
        slot_ref[n + i] = 0
    return n


def fetch_list(wanted, sign, list_hbm, list_ref, count_ref, slot_ref, sem):
    copy = pltpu.make_async_copy(list_hbm, list_ref, sem)
    copy.start()

    def listing():
        copy.wait()
        return list_slots(wanted, sign, list_ref, count_ref, slot_ref)

    return listing


def each_slot(n, slot_ref, hang_hbm, hang_ref, sems, act):
    @pl.loop(0, n)
    def _(k):
        act(pltpu.make_async_copy(hang_hbm.at[slot_ref[k]], hang_ref.at[k], sems.at[k]))


def add_slots(acc, n, list_ref, hang_ref, tr_ref, slot_ref):
    def work(first, size):
        parts = []
        for i in range(size):
            k = first + i
            h = slot_ref[k]
            source = list_ref[0, h] * 6 + list_ref[1, h]
            target = jnp.where(k < n, list_ref[3, h], ELEMS)
            parts.append((target, mm(hang_ref[k], tr_ref[source], TN)))
        for target, part in parts:
            acc[target] += part

    whole = (n + GROUP // 2 - 1) // GROUP

    @pl.loop(0, whole)
    def _(g):
        work(g * GROUP, GROUP)

    @pl.when(n > whole * GROUP)
    def _():
        work(whole * GROUP, GROUP // 2)


def core_and_row():
    return lax.axis_index("c"), lax.axis_index("x") % 2


def flux(weights, tr_ref, e, f):
    return mm(weights, tr_ref[6 * e + f], TN)


def swap_if(flag, a, b):
    return jnp.where(flag, b, a), jnp.where(flag, a, b)


def edge_fluxes(face_ref, tr_ref, ya_ref, yb_ref):
    _, odd = core_and_row()
    for x in range(2):
        for z in range(2):
            up = flux(face_ref[1, x, z], tr_ref, 4 * x + 2 + z, 3)
            down = flux(face_ref[2, x, z], tr_ref, 4 * x + z, 2)
            first, second = swap_if(odd == 1, up, down)
            ya_ref[2 * x + z] = first.astype(jnp.bfloat16)
            yb_ref[2 * x + z] = second.astype(jnp.bfloat16)


def cross_part(acc, out_refs, listing, side, list_ref, face_ref, hang_ref, tr_ref, slot_ref):
    for m in range(4):
        piece = flux(face_ref[0, m // 2, m % 2], tr_ref, m + 4 * side, side)
        acc[m + 4 * (1 - side)] = jnp.where(side == 1, spread_a(piece, 0), spread_a(piece, 1))
        acc[m + 4 * side] = jnp.zeros((BLOCK, RHS), jnp.float32)
    add_slots(acc, listing(), list_ref, hang_ref, tr_ref, slot_ref)
    for i, ref in enumerate(out_refs):
        size = ref.shape[0]
        ref[...] = acc[size * i : size * i + size].astype(ref.dtype)


def first_kernel(
    list_hbm, count_ref, rhs_hbm, inv_hbm, face_hbm, hang_hbm,
    rhs_ref, inv_ref, face_ref, hang_ref, tr_ref, cross_ref, ya_ref, yb_ref,
    acc, app_ref, list_ref, slot_ref, sems, hang_sems,
):
    core, _ = core_and_row()
    copies = []

    def bring(source, target):
        copies.append(pltpu.make_async_copy(source, target, sems.at[len(copies)]))
        copies[-1].start()

    bring(list_hbm, list_ref)
    for e in range(0, ELEMS, 2):
        pair = pl.ds(e, 2)
        bring(rhs_hbm.at[pair], rhs_ref.at[pair])
        bring(inv_hbm.at[pair], inv_ref.at[pair])
    late = len(copies)
    bring(face_hbm.at[core, :, :, core], face_ref.at[0])
    bring(face_hbm.at[:, 1, :, 3], face_ref.at[1])
    bring(face_hbm.at[:, 0, :, 2], face_ref.at[2])
    copies[0].wait()
    n = list_slots(1, 2 * core - 1, list_ref, count_ref, slot_ref)
    each_slot(n, slot_ref, hang_hbm, hang_ref, hang_sems, lambda copy: copy.start())

    def lowered(e):
        if e % 2 == 0:
            copies[e + 1].wait()
            copies[e + 2].wait()
        return rhs_ref[e]

    fill_traces(lowered, inv_ref, tr_ref, app_ref)
    for copy in copies[late:]:
        copy.wait()
    edge_fluxes(face_ref, tr_ref, ya_ref, yb_ref)
    each_slot(n, slot_ref, hang_hbm, hang_ref, hang_sems, lambda copy: copy.wait())
    cross_part(acc, (cross_ref,), lambda: n, core, list_ref, face_ref, hang_ref, tr_ref, slot_ref)


def side_first_kernel(
    list_ref, count_ref, face_hbm, hang_hbm, tr_ref, chip_ref, chip2_ref, face_ref, hang_ref, own_face_ref, own_hang_ref,
    acc, slot_ref, own_slot_ref, sems, hang_sems, own_hang_sems,
):
    core, _ = core_and_row()
    pieces = [
        face_hbm.at[1, :, :, 0], face_hbm.at[0, :, :, 1], face_hbm.at[:, 1, :, 2],
        face_hbm.at[:, 0, :, 3], face_hbm.at[:, :, 1, 4], face_hbm.at[:, :, 0, 5],
    ]
    copies = [pltpu.make_async_copy(face_hbm.at[1 - core, :, :, 1 - core], face_ref.at[0], sems.at[6])]
    copies += [pltpu.make_async_copy(p, own_face_ref.at[f], sems.at[f]) for f, p in enumerate(pieces)]
    copies[0].start()
    n = list_slots(-1, 2 * core - 1, list_ref, count_ref, slot_ref)
    each_slot(n, slot_ref, hang_hbm, hang_ref, hang_sems, lambda copy: copy.start())
    for copy in copies[1:]:
        copy.start()
    own_n = list_slots(0, 1, list_ref, count_ref, own_slot_ref)
    each_slot(own_n, own_slot_ref, hang_hbm, own_hang_ref, own_hang_sems, lambda copy: copy.start())
    copies[0].wait()
    each_slot(n, slot_ref, hang_hbm, hang_ref, hang_sems, lambda copy: copy.wait())
    cross_part(acc, (chip_ref, chip2_ref), lambda: n, 1 - core, list_ref, face_ref, hang_ref, tr_ref, slot_ref)
    for copy in copies[1:]:
        copy.wait()
    each_slot(own_n, own_slot_ref, hang_hbm, own_hang_ref, own_hang_sems, lambda copy: copy.wait())


def side_second_kernel(
    list_hbm, count_ref, face_ref, hang_ref, tr_ref, chip_ref, chip2_ref, acc, slot_ref, list_ref, sem
):
    core, _ = core_and_row()
    listing = fetch_list(-1, 2 * core - 1, list_hbm, list_ref, count_ref, slot_ref, sem)
    cross_part(acc, (chip_ref, chip2_ref), listing, 1 - core, list_ref, face_ref, hang_ref, tr_ref, slot_ref)


def own_part(listing, list_ref, face_ref, hang_ref, tr_ref, own_ref, acc, slot_ref):
    for e in range(ELEMS):
        x, y, z = (e >> 2) & 1, (e >> 1) & 1, e & 1
        from_x = flux(face_ref[x, y, z], tr_ref, e ^ 4, x)
        from_y = flux(face_ref[2 + y, x, z], tr_ref, e ^ 2, 2 + y)
        from_z = flux(face_ref[4 + z, x, y], tr_ref, e ^ 1, 4 + z)
        acc[e] = spread_a(from_x, 1 - x) + spread_b(from_y, 1 - y)
        acc[e, face_c(1 - z), :] += from_z
    add_slots(acc, listing(), list_ref, hang_ref, tr_ref, slot_ref)
    own_ref[...] = acc[0:ELEMS]


def own_kernel(list_hbm, count_ref, face_ref, hang_ref, tr_ref, own_ref, acc, slot_ref, list_ref, sem):
    listing = fetch_list(0, 1, list_hbm, list_ref, count_ref, slot_ref, sem)
    own_part(listing, list_ref, face_ref, hang_ref, tr_ref, own_ref, acc, slot_ref)


def inner(e, *pairs):
    return [jnp.sum((a[e].astype(jnp.float32) * b[e].astype(jnp.float32)).reshape(BLOCK // 8, 8, RHS), axis=0) for a, b in pairs]


def gram_rows(*pairs):
    totals = inner(0, *pairs)
    for e in range(1, ELEMS):
        totals = [t + p for t, p in zip(totals, inner(e, *pairs))]
    rows = [jnp.sum(t, axis=0, keepdims=True) for t in totals]
    return jnp.concatenate(rows, axis=1)


def own_gram_kernel(
    list_hbm, count_ref, face_ref, hang_ref, tr_ref, rhs_ref, w1_ref, own_ref, gram_ref, acc, slot_ref, list_ref, sem
):
    listing = fetch_list(0, 1, list_hbm, list_ref, count_ref, slot_ref, sem)
    own_part(listing, list_ref, face_ref, hang_ref, tr_ref, own_ref, acc, slot_ref)
    gram_ref[...] = gram_rows((rhs_ref, rhs_ref), (rhs_ref, w1_ref), (w1_ref, w1_ref))


def landed(e, own_ref, cross_ref, chip_refs, ya_ref, yb_ref):
    _, odd = core_and_row()
    y = (e >> 1) & 1
    n = 2 * (e >> 2) + (e & 1)
    edge = swap_if(odd == 1, ya_ref[n].astype(jnp.float32), yb_ref[n].astype(jnp.float32))[1 - y]
    came = cross_ref[e].astype(jnp.float32) + chip_refs[e // 4][e % 4].astype(jnp.float32)
    return own_ref[e] + came + spread_b(edge, y)


def second_kernel(
    list_hbm, count_ref, own_ref, in_cross, in_chip, in_chip2, in_ya, in_yb, inv_ref, face_ref, hang_ref,
    w_ref, tr_ref, cross_ref, ya_ref, yb_ref, acc, app_ref, slot_ref, list_ref, sem,
):
    core, _ = core_and_row()
    listing = fetch_list(1, 2 * core - 1, list_hbm, list_ref, count_ref, slot_ref, sem)

    def lowered(e):
        w = landed(e, own_ref, in_cross, (in_chip, in_chip2), in_ya, in_yb)
        w_ref[e] = w
        return w.astype(jnp.bfloat16)

    fill_traces(lowered, inv_ref, tr_ref, app_ref)
    edge_fluxes(face_ref, tr_ref, ya_ref, yb_ref)
    cross_part(acc, (cross_ref,), listing, core, list_ref, face_ref, hang_ref, tr_ref, slot_ref)


def last_kernel(own_ref, in_cross, in_chip, in_chip2, in_ya, in_yb, rhs_ref, w1_ref, early_ref, w_ref, keep_ref, give_ref):
    for e in range(ELEMS):
        w_ref[e] = landed(e, own_ref, in_cross, (in_chip, in_chip2), in_ya, in_yb)
    late = gram_rows((rhs_ref, w_ref), (w1_ref, w_ref), (w_ref, w_ref))
    early = early_ref[...]
    core, _ = core_and_row()
    keep_ref[...] = jnp.where(core == 0, early, late)
    give_ref[...] = jnp.where(core == 0, late, early)


def combine_kernel(entries, mine_ref, other_ref, rhs_ref, w1_ref, w2_ref, out_hbm, hess_ref, out_ref, sems):
    core, _ = core_and_row()
    mine = mine_ref[...] * (1.0 / entries)
    other = other_ref[...] * (1.0 / entries)
    early = jnp.where(core == 0, mine, other)
    late = jnp.where(core == 0, other, mine)
    g00, g01, g11 = (early[:, RHS * i : RHS * i + RHS] for i in range(3))
    g02, g12, g22 = (late[:, RHS * i : RHS * i + RHS] for i in range(3))
    norm0 = g00 + EPS
    size0 = jnp.sqrt(norm0)
    h11 = (g00 + g01) / norm0
    c1 = (EPS - g01) / norm0
    square1 = jnp.maximum(g11 + 2.0 * c1 * g01 + c1 * c1 * g00, 0.0) / norm0 + EPS
    h21 = jnp.sqrt(square1)
    s2 = 1.0 / (size0 * h21)
    ratio = (g02 + c1 * g01 + EPS * h11) / norm0
    h12 = ratio * s2 * size0
    q = EPS / square1 - s2 * s2 * (g12 + c1 * (g11 + g02 + c1 * g01))
    h22 = 1.0 - q
    alpha = c1 + q
    beta = c1 * q - ratio
    total = g22 + 2.0 * (alpha * g12 + beta * g02 + alpha * beta * g01)
    total = total + alpha * alpha * g11 + beta * beta * g00
    h32 = jnp.sqrt(s2 * s2 * jnp.maximum(total, 0.0) + EPS)
    zero = jnp.zeros_like(h11)
    for i, row in enumerate(((h11, h12), (h21, h22), (zero, h32))):
        hess_ref[i] = jnp.concatenate(row, axis=0)
    k2 = s2 / h32
    k1 = k2 * alpha
    k0 = k2 * beta
    copies = []
    for e in range(ELEMS):
        out_ref[e] = k2 * w2_ref[e] + k1 * w1_ref[e] + k0 * rhs_ref[e].astype(jnp.float32)
        copies.append(pltpu.make_async_copy(out_ref.at[e], out_hbm.at[e], sems.at[e]))
        copies[e].start()
    for copy in copies:
        copy.wait()


def shape(dims, dtype=jnp.float32):
    return jax.ShapeDtypeStruct(dims, dtype)


FIELD = (ELEMS, BLOCK, RHS)
TRACES = (6 * ELEMS, FACE, RHS)
SIDE = (4, FACE, RHS)
HALF = (4, BLOCK, RHS)
SMEM = pl.BlockSpec(memory_space=pltpu.SMEM)
VMEM = pl.BlockSpec(memory_space=pltpu.VMEM)
HBM = pl.BlockSpec(memory_space=pltpu.HBM)


def call(kernel, in_specs, outs, scratch, flops, moved, out_specs=None):
    return pl.pallas_call(
        kernel,
        out_shape=outs,
        in_specs=in_specs,
        out_specs=out_specs or [VMEM] * len(outs),
        scratch_shapes=scratch,
        compiler_params=pltpu.CompilerParams(vmem_limit_bytes=VMEM_LIMIT),
        cost_estimate=pl.CostEstimate(flops=flops, bytes_accessed=moved, transcendentals=0),
    )


def stay(x):
    return pltpu.with_memory_space_constraint(x, pltpu.HBM)


def per_device(entries, pairs, rhs_field, inv_block, face_block, hang_list, hang_count, hang_block):
    rows = stay(hang_list.reshape(HANG, 4).T)
    count = hang_count
    field = pltpu.VMEM(FIELD, jnp.float32)
    acc = pltpu.VMEM((ELEMS + 1, BLOCK, RHS), jnp.float32)
    slots = pltpu.SMEM((HANG + 8,), jnp.int32)
    bf16 = jnp.bfloat16
    million = 10**6
    scalars = [SMEM, SMEM]
    later = [HBM, SMEM]
    lists = [slots, pltpu.SMEM((4, HANG), jnp.int32), pltpu.SemaphoreType.DMA]
    sems = lambda n: pltpu.SemaphoreType.DMA((n,))
    faces = stay(face_block)
    hangs = stay(hang_block.reshape(HANG, FACE, BLOCK))
    packed = shape((HANG, FACE, BLOCK), bf16)
    held = lambda n: shape((n, 2, 2, FACE, FACE), bf16)
    halves = [shape(HALF, bf16)] * 2
    sent = [shape(TRACES, bf16), shape(FIELD, bf16), shape(SIDE, bf16), shape(SIDE, bf16)]

    rhs, inv, face, hang, traces, *out = call(
        first_kernel, [HBM, SMEM] + [HBM] * 4, [shape(FIELD, bf16), shape((ELEMS, BLOCK, BLOCK), bf16), held(3), packed] + sent,
        [
            acc, field, pltpu.SMEM((4, HANG), jnp.int32), slots,
            sems(ELEMS + 4), sems(HANG),
        ],
        300 * million, 6 * million,
    )(rows, count, stay(rhs_field.reshape(FIELD)), stay(inv_block.reshape(ELEMS, BLOCK, BLOCK)), faces, hangs)

    def exchange(out, side_call, own_call):
        cross, ya, yb = out
        in_cross = lax.ppermute(cross, ("z", "y", "c"), pairs["cross"])
        in_ya = lax.ppermute(ya, "x", pairs["even"])
        in_yb = lax.ppermute(yb, "x", pairs["odd"])
        low, high, *weights = side_call()
        in_chip = [lax.ppermute(part, "c", [(0, 1), (1, 0)]) for part in (low, high)]
        own, *rest = own_call(weights[2:])
        return (own, in_cross, *in_chip, in_ya, in_yb), weights, rest

    def side_first():
        return call(
            side_first_kernel, scalars + [HBM, HBM, VMEM], halves + [held(1), packed, held(6), packed],
            [acc, slots, slots, sems(7), sems(HANG), sems(HANG)], SIDE_FLOPS, 4 * million,
        )(rows, count, faces, hangs, traces)

    def own_first(weights):
        return call(own_kernel, later + [VMEM] * 3, [shape(FIELD)], [acc, *lists], OWN_FLOPS, 6 * million)(
            rows, count, *weights, traces
        )

    arrived, weights, _ = exchange(out, side_first, own_first)
    w1, traces, *out = call(
        second_kernel, later + [VMEM] * 9, [shape(FIELD)] + sent, [acc, field, *lists], 300 * million, 8 * million,
    )(rows, count, *arrived, inv, face, hang)

    def side_second():
        return call(side_second_kernel, later + [VMEM] * 3, halves, [acc, *lists], SIDE_FLOPS, 4 * million)(
            rows, count, *weights[:2], traces
        )

    def own_second(_):
        return call(
            own_gram_kernel, later + [VMEM] * 5, [shape(FIELD), shape((1, 3 * RHS))], [acc, *lists],
            OWN_FLOPS, 6 * million,
        )(rows, count, *weights[2:], traces, rhs, w1)

    arrived, _, (early,) = exchange(out, side_second, own_second)
    w2, keep, give = call(
        last_kernel, [VMEM] * 9, [shape(FIELD), shape((1, 3 * RHS)), shape((1, 3 * RHS))], [], 10 * million, 8 * million
    )(*arrived, rhs, w1, early)

    swap = [(0, 1), (1, 0)]
    part = keep + lax.ppermute(give, "c", swap)
    chips = lax.axis_size(("z", "y", "x"))
    mine = lax.all_to_all(jnp.broadcast_to(part, (chips, 1, 3 * RHS)), ("z", "y", "x"), 0, 0).sum(0)
    last, hessenberg = call(
        functools.partial(combine_kernel, entries), [VMEM] * 5, [shape(FIELD), shape((3, 2, RHS))],
        [field, pltpu.SemaphoreType.DMA((ELEMS,))], 10 * million, 6 * million, [HBM, VMEM],
    )(mine, lax.ppermute(mine, "c", swap), rhs, w1, w2)
    return last.reshape(rhs_field.shape), hessenberg


def solution(mesh):
    count_x, count_y = mesh.shape["gx"], mesh.shape["gy"]
    grid = jax.sharding.Mesh(
        mesh.devices.reshape(CHIPS_Z, CHIPS_Y, 2, count_y), ("z", "y", "c", "x")
    )
    pairs = {"cross": [], "even": [], "odd": []}
    for i in range(1, count_x - 1, 2):
        pairs["cross"] += [(i, i + 1), (i + 1, i)]
    for j in range(count_y - 1):
        pairs["odd" if j % 2 else "even"] += [(j, j + 1), (j + 1, j)]
    long = ("z", "y", "c")
    in_specs = (P(long, "x"),) * 6
    out_specs = (P(long, "x"), P())
    entries = float(ELEMS * BLOCK * count_x * count_y)
    return jax.shard_map(
        functools.partial(per_device, entries, pairs),
        mesh=grid, in_specs=in_specs, out_specs=out_specs, check_vma=False,
    )
```

```python
import functools

import jax
import jax.numpy as jnp
from jax import lax
from jax.experimental import pallas as pl
from jax.experimental.pallas import tpu as pltpu
from jax.sharding import PartitionSpec as P

VARS = 5
CHIPS_Z = 8
CHIPS_Y = 4
BLOCK = 320
FACE = 80
ELEMS = 8
RHS = 128
HANG = 32
EPS = 1e-6
GROUP = 8
SIDE_FLOPS = 100 * 10**6
OWN_FLOPS = 4000 * 10**6
NEAR_FLOPS = 10**6
VMEM_LIMIT = 40 * 1024 * 1024

TN = (((0,), (0,)), ((), ()))
NN = (((1,), (0,)), ((), ()))


def mm(a, b, dims):
    return lax.dot_general(a, b, dims, preferred_element_type=jnp.float32)


def low_half():
    return lax.broadcasted_iota(jnp.int32, (10, 8, RHS), 1) < 4


def turn(x):
    return pltpu.roll(x, 4, 1)


def trace_a(field, end):
    return field.reshape(VARS, 4, 16, RHS)[:, 3 * end].reshape(FACE, RHS)


def trace_b(field, end):
    rows = field.reshape(10, 4, 8, RHS)
    if end == 0:
        out = jnp.where(low_half(), rows[:, 0], turn(rows[:, 2]))
    else:
        out = jnp.where(low_half(), turn(rows[:, 1]), rows[:, 3])
    return out.reshape(FACE, RHS)


def spread_a(values, end):
    piece = values.reshape(VARS, 1, 16, RHS)
    zero = jnp.zeros((VARS, 3, 16, RHS), jnp.float32)
    return jnp.concatenate([zero, piece] if end else [piece, zero], axis=1).reshape(BLOCK, RHS)


def spread_b(values, end):
    rows = values.reshape(10, 8, RHS)
    zero = jnp.zeros_like(rows)
    low = low_half()
    if end == 0:
        parts = [jnp.where(low, rows, 0.0), zero, jnp.where(low, turn(rows), 0.0), zero]
    else:
        parts = [zero, jnp.where(low, 0.0, turn(rows)), zero, jnp.where(low, 0.0, rows)]
    return jnp.stack(parts, axis=1).reshape(BLOCK, RHS)


def face_c(end):
    return pl.ds(3 * end, FACE, stride=4)


def fill_traces(lowered, inv_ref, tr_ref, app_ref):
    for e in range(ELEMS):
        field = lowered(e)
        applied = mm(inv_ref[e], field, TN)
        app_ref[e] = applied
        for end in range(2):
            tr_ref[6 * e + end] = trace_a(applied, end).astype(jnp.bfloat16)
            tr_ref[6 * e + 2 + end] = trace_b(applied, end).astype(jnp.bfloat16)
            tr_ref[6 * e + 4 + end] = app_ref[e, face_c(end), :].astype(jnp.bfloat16)


def list_slots(wanted, sign, list_ref, count_ref, slot_ref):
    live = count_ref[0, 0]

    def look(h, n):
        slot_ref[n] = h
        hit = jnp.logical_and(list_ref[2, h] * sign == wanted, h < live)
        return n + hit.astype(jnp.int32)

    n = lax.fori_loop(0, HANG, look, jnp.int32(0), unroll=8)
    for i in range(GROUP):
        slot_ref[n + i] = 0
    return n


def fetch_list(wanted, sign, list_hbm, list_ref, count_ref, slot_ref, sem):
    copy = pltpu.make_async_copy(list_hbm, list_ref, sem)
    copy.start()

    def listing():
        copy.wait()
        return list_slots(wanted, sign, list_ref, count_ref, slot_ref)

    return listing


def each_slot(n, slot_ref, hang_hbm, hang_ref, sems, act):
    @pl.loop(0, n)
    def _(k):
        act(pltpu.make_async_copy(hang_hbm.at[slot_ref[k]], hang_ref.at[k], sems.at[k]))


def add_slots(acc, n, list_ref, hang_ref, tr_ref, slot_ref):
    def work(first, size):
        parts = []
        for i in range(size):
            k = first + i
            h = slot_ref[k]
            source = list_ref[0, h] * 6 + list_ref[1, h]
            target = jnp.where(k < n, list_ref[3, h], ELEMS)
            parts.append((target, mm(hang_ref[k], tr_ref[source], TN)))
        for target, part in parts:
            acc[target] += part

    whole = (n + GROUP // 2 - 1) // GROUP

    @pl.loop(0, whole)
    def _(g):
        work(g * GROUP, GROUP)

    @pl.when(n > whole * GROUP)
    def _():
        work(whole * GROUP, GROUP // 2)


def core_and_row():
    return lax.axis_index("c"), lax.axis_index("x") % 2


def flux(weights, tr_ref, e, f):
    return mm(weights, tr_ref[6 * e + f], TN)


def swap_if(flag, a, b):
    return jnp.where(flag, b, a), jnp.where(flag, a, b)


def edge_fluxes(face_ref, tr_ref, ya_ref, yb_ref):
    _, odd = core_and_row()
    for x in range(2):
        for z in range(2):
            up = flux(face_ref[1, x, z], tr_ref, 4 * x + 2 + z, 3)
            down = flux(face_ref[2, x, z], tr_ref, 4 * x + z, 2)
            first, second = swap_if(odd == 1, up, down)
            ya_ref[2 * x + z] = first.astype(jnp.bfloat16)
            yb_ref[2 * x + z] = second.astype(jnp.bfloat16)


def cross_part(acc, out_refs, listing, side, list_ref, face_ref, hang_ref, tr_ref, slot_ref):
    for m in range(4):
        piece = flux(face_ref[0, m // 2, m % 2], tr_ref, m + 4 * side, side)
        acc[m + 4 * (1 - side)] = jnp.where(side == 1, spread_a(piece, 0), spread_a(piece, 1))
        acc[m + 4 * side] = jnp.zeros((BLOCK, RHS), jnp.float32)
    add_slots(acc, listing(), list_ref, hang_ref, tr_ref, slot_ref)
    for i, ref in enumerate(out_refs):
        size = ref.shape[0]
        ref[...] = acc[size * i : size * i + size].astype(ref.dtype)


def first_kernel(
    list_hbm, count_ref, rhs_hbm, inv_hbm, face_hbm, hang_hbm,
    rhs_ref, inv_ref, face_ref, hang_ref, tr_ref, cross_ref,
    acc, app_ref, list_ref, slot_ref, sems, hang_sems,
):
    core, _ = core_and_row()
    copies = []

    def bring(source, target):
        copies.append(pltpu.make_async_copy(source, target, sems.at[len(copies)]))
        copies[-1].start()

    bring(list_hbm, list_ref)
    for e in range(0, ELEMS, 2):
        pair = pl.ds(e, 2)
        bring(rhs_hbm.at[pair], rhs_ref.at[pair])
        bring(inv_hbm.at[pair], inv_ref.at[pair])
    late = len(copies)
    bring(face_hbm.at[core, :, :, core], face_ref.at[0])
    copies[0].wait()
    n = list_slots(1, 2 * core - 1, list_ref, count_ref, slot_ref)
    each_slot(n, slot_ref, hang_hbm, hang_ref, hang_sems, lambda copy: copy.start())

    def lowered(e):
        if e % 2 == 0:
            copies[e + 1].wait()
            copies[e + 2].wait()
        return rhs_ref[e]

    fill_traces(lowered, inv_ref, tr_ref, app_ref)
    for copy in copies[late:]:
        copy.wait()
    each_slot(n, slot_ref, hang_hbm, hang_ref, hang_sems, lambda copy: copy.wait())
    cross_part(acc, (cross_ref,), lambda: n, core, list_ref, face_ref, hang_ref, tr_ref, slot_ref)


def side_first_kernel(
    list_hbm, count_ref, face_hbm, hang_hbm, tr_ref, chip_ref, chip2_ref, ya_ref, yb_ref, face_ref, hang_ref, own_face_ref, own_hang_ref,
    acc, slot_ref, list_ref, list_sem, own_slot_ref, sems, hang_sems, own_hang_sems,
):
    core, _ = core_and_row()
    listing = fetch_list(-1, 2 * core - 1, list_hbm, list_ref, count_ref, slot_ref, list_sem)
    pieces = [
        face_hbm.at[1, :, :, 0], face_hbm.at[0, :, :, 1], face_hbm.at[:, 1, :, 2],
        face_hbm.at[:, 0, :, 3], face_hbm.at[:, :, 1, 4], face_hbm.at[:, :, 0, 5],
    ]
    mine = [face_hbm.at[1 - core, :, :, 1 - core], face_hbm.at[:, 1, :, 3], face_hbm.at[:, 0, :, 2]]
    copies = [pltpu.make_async_copy(p, face_ref.at[f], sems.at[6 + f]) for f, p in enumerate(mine)]
    copies += [pltpu.make_async_copy(p, own_face_ref.at[f], sems.at[f]) for f, p in enumerate(pieces)]
    for copy in copies[:3]:
        copy.start()
    n = listing()
    each_slot(n, slot_ref, hang_hbm, hang_ref, hang_sems, lambda copy: copy.start())
    for copy in copies[3:]:
        copy.start()
    own_n = list_slots(0, 1, list_ref, count_ref, own_slot_ref)
    each_slot(own_n, own_slot_ref, hang_hbm, own_hang_ref, own_hang_sems, lambda copy: copy.start())
    for copy in copies[:3]:
        copy.wait()
    edge_fluxes(face_ref, tr_ref, ya_ref, yb_ref)
    each_slot(n, slot_ref, hang_hbm, hang_ref, hang_sems, lambda copy: copy.wait())
    cross_part(acc, (chip_ref, chip2_ref), lambda: n, 1 - core, list_ref, face_ref, hang_ref, tr_ref, slot_ref)
    for copy in copies[3:]:
        copy.wait()
    each_slot(own_n, own_slot_ref, hang_hbm, own_hang_ref, own_hang_sems, lambda copy: copy.wait())


def side_second_kernel(
    list_hbm, count_ref, face_ref, hang_ref, tr_ref, chip_ref, chip2_ref, ya_ref, yb_ref, acc, slot_ref, list_ref, sem
):
    core, _ = core_and_row()
    listing = fetch_list(-1, 2 * core - 1, list_hbm, list_ref, count_ref, slot_ref, sem)
    edge_fluxes(face_ref, tr_ref, ya_ref, yb_ref)
    cross_part(acc, (chip_ref, chip2_ref), listing, 1 - core, list_ref, face_ref, hang_ref, tr_ref, slot_ref)


def own_part(listing, list_ref, face_ref, hang_ref, tr_ref, own_ref, acc, slot_ref):
    for e in range(ELEMS):
        x, y, z = (e >> 2) & 1, (e >> 1) & 1, e & 1
        from_x = flux(face_ref[x, y, z], tr_ref, e ^ 4, x)
        from_y = flux(face_ref[2 + y, x, z], tr_ref, e ^ 2, 2 + y)
        from_z = flux(face_ref[4 + z, x, y], tr_ref, e ^ 1, 4 + z)
        acc[e] = spread_a(from_x, 1 - x) + spread_b(from_y, 1 - y)
        acc[e, face_c(1 - z), :] += from_z
    add_slots(acc, listing(), list_ref, hang_ref, tr_ref, slot_ref)
    own_ref[...] = acc[0:ELEMS]


def own_kernel(list_hbm, count_ref, face_ref, hang_ref, tr_ref, own_ref, acc, slot_ref, list_ref, sem):
    listing = fetch_list(0, 1, list_hbm, list_ref, count_ref, slot_ref, sem)
    own_part(listing, list_ref, face_ref, hang_ref, tr_ref, own_ref, acc, slot_ref)


def inner(e, *pairs):
    return [jnp.sum((a[e].astype(jnp.float32) * b[e].astype(jnp.float32)).reshape(BLOCK // 8, 8, RHS), axis=0) for a, b in pairs]


def gram_rows(*pairs):
    totals = inner(0, *pairs)
    for e in range(1, ELEMS):
        totals = [t + p for t, p in zip(totals, inner(e, *pairs))]
    rows = [jnp.sum(t, axis=0, keepdims=True) for t in totals]
    return jnp.concatenate(rows, axis=1)


def own_gram_kernel(
    list_hbm, count_ref, face_ref, hang_ref, tr_ref, rhs_ref, w1_ref, own_ref, gram_ref, acc, slot_ref, list_ref, sem
):
    listing = fetch_list(0, 1, list_hbm, list_ref, count_ref, slot_ref, sem)
    own_part(listing, list_ref, face_ref, hang_ref, tr_ref, own_ref, acc, slot_ref)
    gram_ref[...] = gram_rows((rhs_ref, rhs_ref), (rhs_ref, w1_ref), (w1_ref, w1_ref))


def near_kernel(own_ref, chip_ref, chip2_ref, ya_ref, yb_ref, near_ref):
    _, odd = core_and_row()
    for e in range(ELEMS):
        y = (e >> 1) & 1
        n = 2 * (e >> 2) + (e & 1)
        edge = swap_if(odd == 1, ya_ref[n].astype(jnp.float32), yb_ref[n].astype(jnp.float32))[1 - y]
        chip = (chip_ref, chip2_ref)[e // 4][e % 4].astype(jnp.float32)
        near_ref[e] = own_ref[e] + chip + spread_b(edge, y)


def landed(e, near_ref, cross_ref):
    return near_ref[e] + cross_ref[e].astype(jnp.float32)


def second_kernel(
    list_hbm, count_ref, near_ref, in_cross, inv_ref, face_ref, hang_ref,
    w_ref, tr_ref, cross_ref, acc, app_ref, slot_ref, list_ref, sem,
):
    core, _ = core_and_row()
    listing = fetch_list(1, 2 * core - 1, list_hbm, list_ref, count_ref, slot_ref, sem)

    def lowered(e):
        w = landed(e, near_ref, in_cross)
        w_ref[e] = w
        return w.astype(jnp.bfloat16)

    fill_traces(lowered, inv_ref, tr_ref, app_ref)
    cross_part(acc, (cross_ref,), listing, core, list_ref, face_ref, hang_ref, tr_ref, slot_ref)


def last_kernel(near_ref, in_cross, rhs_ref, w1_ref, early_ref, w_ref, keep_ref, give_ref):
    for e in range(ELEMS):
        w_ref[e] = landed(e, near_ref, in_cross)
    late = gram_rows((rhs_ref, w_ref), (w1_ref, w_ref), (w_ref, w_ref))
    early = early_ref[...]
    core, _ = core_and_row()
    keep_ref[...] = jnp.where(core == 0, early, late)
    give_ref[...] = jnp.where(core == 0, late, early)


def combine_kernel(entries, mine_ref, other_ref, rhs_ref, w1_ref, w2_ref, out_hbm, hess_ref, out_ref, sems):
    core, _ = core_and_row()
    mine = mine_ref[...] * (1.0 / entries)
    other = other_ref[...] * (1.0 / entries)
    early = jnp.where(core == 0, mine, other)
    late = jnp.where(core == 0, other, mine)
    g00, g01, g11 = (early[:, RHS * i : RHS * i + RHS] for i in range(3))
    g02, g12, g22 = (late[:, RHS * i : RHS * i + RHS] for i in range(3))
    norm0 = g00 + EPS
    size0 = jnp.sqrt(norm0)
    h11 = (g00 + g01) / norm0
    c1 = (EPS - g01) / norm0
    square1 = jnp.maximum(g11 + 2.0 * c1 * g01 + c1 * c1 * g00, 0.0) / norm0 + EPS
    h21 = jnp.sqrt(square1)
    s2 = 1.0 / (size0 * h21)
    ratio = (g02 + c1 * g01 + EPS * h11) / norm0
    h12 = ratio * s2 * size0
    q = EPS / square1 - s2 * s2 * (g12 + c1 * (g11 + g02 + c1 * g01))
    h22 = 1.0 - q
    alpha = c1 + q
    beta = c1 * q - ratio
    total = g22 + 2.0 * (alpha * g12 + beta * g02 + alpha * beta * g01)
    total = total + alpha * alpha * g11 + beta * beta * g00
    h32 = jnp.sqrt(s2 * s2 * jnp.maximum(total, 0.0) + EPS)
    zero = jnp.zeros_like(h11)
    for i, row in enumerate(((h11, h12), (h21, h22), (zero, h32))):
        hess_ref[i] = jnp.concatenate(row, axis=0)
    k2 = s2 / h32
    k1 = k2 * alpha
    k0 = k2 * beta
    copies = []
    for e in range(ELEMS):
        out_ref[e] = k2 * w2_ref[e] + k1 * w1_ref[e] + k0 * rhs_ref[e].astype(jnp.float32)
        copies.append(pltpu.make_async_copy(out_ref.at[e], out_hbm.at[e], sems.at[e]))
        copies[e].start()
    for copy in copies:
        copy.wait()


def shape(dims, dtype=jnp.float32):
    return jax.ShapeDtypeStruct(dims, dtype)


FIELD = (ELEMS, BLOCK, RHS)
TRACES = (6 * ELEMS, FACE, RHS)
SIDE = (4, FACE, RHS)
HALF = (4, BLOCK, RHS)
SMEM = pl.BlockSpec(memory_space=pltpu.SMEM)
VMEM = pl.BlockSpec(memory_space=pltpu.VMEM)
HBM = pl.BlockSpec(memory_space=pltpu.HBM)


def call(kernel, in_specs, outs, scratch, flops, moved, out_specs=None):
    return pl.pallas_call(
        kernel,
        out_shape=outs,
        in_specs=in_specs,
        out_specs=out_specs or [VMEM] * len(outs),
        scratch_shapes=scratch,
        compiler_params=pltpu.CompilerParams(vmem_limit_bytes=VMEM_LIMIT),
        cost_estimate=pl.CostEstimate(flops=flops, bytes_accessed=moved, transcendentals=0),
    )


def stay(x):
    return pltpu.with_memory_space_constraint(x, pltpu.HBM)


def per_device(entries, pairs, rhs_field, inv_block, face_block, hang_list, hang_count, hang_block):
    rows = stay(hang_list.reshape(HANG, 4).T)
    count = hang_count
    field = pltpu.VMEM(FIELD, jnp.float32)
    acc = pltpu.VMEM((ELEMS + 1, BLOCK, RHS), jnp.float32)
    slots = pltpu.SMEM((HANG + 8,), jnp.int32)
    bf16 = jnp.bfloat16
    million = 10**6
    later = [HBM, SMEM]
    lists = [slots, pltpu.SMEM((4, HANG), jnp.int32), pltpu.SemaphoreType.DMA]
    sems = lambda n: pltpu.SemaphoreType.DMA((n,))
    faces = stay(face_block)
    hangs = stay(hang_block.reshape(HANG, FACE, BLOCK))
    packed = shape((HANG, FACE, BLOCK), bf16)
    held = lambda n: shape((n, 2, 2, FACE, FACE), bf16)
    sent = [shape(TRACES, bf16), shape(FIELD, bf16)]
    beside = [shape(HALF, bf16)] * 2 + [shape(SIDE, bf16)] * 2

    rhs, inv, face, hang, traces, cross = call(
        first_kernel, [HBM, SMEM] + [HBM] * 4, [shape(FIELD, bf16), shape((ELEMS, BLOCK, BLOCK), bf16), held(1), packed] + sent,
        [
            acc, field, pltpu.SMEM((4, HANG), jnp.int32), slots,
            sems(ELEMS + 2), sems(HANG),
        ],
        300 * million, 6 * million,
    )(rows, count, stay(rhs_field.reshape(FIELD)), stay(inv_block.reshape(ELEMS, BLOCK, BLOCK)), faces, hangs)

    def exchange(cross, side_call, own_call):
        in_cross = lax.ppermute(cross, ("z", "y", "c"), pairs["cross"])
        low, high, ya, yb, *weights = side_call()
        in_ya = lax.ppermute(ya, "x", pairs["even"])
        in_yb = lax.ppermute(yb, "x", pairs["odd"])
        in_chip = [lax.ppermute(part, "c", [(0, 1), (1, 0)]) for part in (low, high)]
        own, *rest = own_call(weights[2:])
        near = call(near_kernel, [VMEM] * 5, [shape(FIELD)], [], NEAR_FLOPS, 6 * million)(own, *in_chip, in_ya, in_yb)[0]
        return (near, in_cross), weights, rest

    def side_first():
        return call(
            side_first_kernel, later + [HBM, HBM, VMEM], beside + [held(3), packed, held(6), packed],
            [acc, *lists, slots, sems(9), sems(HANG), sems(HANG)], SIDE_FLOPS, 4 * million,
        )(rows, count, faces, hangs, traces)

    def own_first(weights):
        return call(own_kernel, later + [VMEM] * 3, [shape(FIELD)], [acc, *lists], OWN_FLOPS, 6 * million)(
            rows, count, *weights, traces
        )

    arrived, weights, _ = exchange(cross, side_first, own_first)
    w1, traces, cross = call(
        second_kernel, later + [VMEM] * 5, [shape(FIELD)] + sent, [acc, field, *lists], 300 * million, 8 * million,
    )(rows, count, *arrived, inv, face, hang)

    def side_second():
        return call(side_second_kernel, later + [VMEM] * 3, beside, [acc, *lists], SIDE_FLOPS, 4 * million)(
            rows, count, *weights[:2], traces
        )

    def own_second(_):
        return call(
            own_gram_kernel, later + [VMEM] * 5, [shape(FIELD), shape((1, 3 * RHS))], [acc, *lists],
            OWN_FLOPS, 6 * million,
        )(rows, count, *weights[2:], traces, rhs, w1)

    arrived, _, (early,) = exchange(cross, side_second, own_second)
    w2, keep, give = call(
        last_kernel, [VMEM] * 5, [shape(FIELD), shape((1, 3 * RHS)), shape((1, 3 * RHS))], [], 10 * million, 8 * million
    )(*arrived, rhs, w1, early)

    swap = [(0, 1), (1, 0)]
    part = keep + lax.ppermute(give, "c", swap)
    chips = lax.axis_size(("z", "y", "x"))
    mine = lax.all_to_all(jnp.broadcast_to(part, (chips, 1, 3 * RHS)), ("z", "y", "x"), 0, 0).sum(0)
    last, hessenberg = call(
        functools.partial(combine_kernel, entries), [VMEM] * 5, [shape(FIELD), shape((3, 2, RHS))],
        [field, pltpu.SemaphoreType.DMA((ELEMS,))], 10 * million, 6 * million, [HBM, VMEM],
    )(mine, lax.ppermute(mine, "c", swap), rhs, w1, w2)
    return last.reshape(rhs_field.shape), hessenberg


def solution(mesh):
    count_x, count_y = mesh.shape["gx"], mesh.shape["gy"]
    grid = jax.sharding.Mesh(
        mesh.devices.reshape(CHIPS_Z, CHIPS_Y, 2, count_y), ("z", "y", "c", "x")
    )
    pairs = {"cross": [], "even": [], "odd": []}
    for i in range(1, count_x - 1, 2):
        pairs["cross"] += [(i, i + 1), (i + 1, i)]
    for j in range(count_y - 1):
        pairs["odd" if j % 2 else "even"] += [(j, j + 1), (j + 1, j)]
    long = ("z", "y", "c")
    in_specs = (P(long, "x"),) * 6
    out_specs = (P(long, "x"), P())
    entries = float(ELEMS * BLOCK * count_x * count_y)
    return jax.shard_map(
        functools.partial(per_device, entries, pairs),
        mesh=grid, in_specs=in_specs, out_specs=out_specs, check_vma=False,
    )
```

```python
import functools

import jax
import jax.numpy as jnp
from jax import lax
from jax.experimental import pallas as pl
from jax.experimental.pallas import tpu as pltpu
from jax.sharding import PartitionSpec as P

VARS = 5
CHIPS_Z = 8
CHIPS_Y = 4
BLOCK = 320
FACE = 80
ELEMS = 8
RHS = 128
HANG = 32
EPS = 1e-6
GROUP = 8
SIDE_FLOPS = 100 * 10**6
OWN_FLOPS = 4000 * 10**6
NEAR_FLOPS = 10**6
VMEM_LIMIT = 40 * 1024 * 1024

TN = (((0,), (0,)), ((), ()))
NN = (((1,), (0,)), ((), ()))


def mm(a, b, dims):
    return lax.dot_general(a, b, dims, preferred_element_type=jnp.float32)


def low_half():
    return lax.broadcasted_iota(jnp.int32, (10, 8, RHS), 1) < 4


def turn(x):
    return pltpu.roll(x, 4, 1)


def trace_a(field, end):
    return field.reshape(VARS, 4, 16, RHS)[:, 3 * end].reshape(FACE, RHS)


def trace_b(field, end):
    rows = field.reshape(10, 4, 8, RHS)
    if end == 0:
        out = jnp.where(low_half(), rows[:, 0], turn(rows[:, 2]))
    else:
        out = jnp.where(low_half(), turn(rows[:, 1]), rows[:, 3])
    return out.reshape(FACE, RHS)


def spread_a(values, end):
    piece = values.reshape(VARS, 1, 16, RHS)
    zero = jnp.zeros((VARS, 3, 16, RHS), jnp.float32)
    return jnp.concatenate([zero, piece] if end else [piece, zero], axis=1).reshape(BLOCK, RHS)


def spread_b(values, end):
    rows = values.reshape(10, 8, RHS)
    zero = jnp.zeros_like(rows)
    low = low_half()
    if end == 0:
        parts = [jnp.where(low, rows, 0.0), zero, jnp.where(low, turn(rows), 0.0), zero]
    else:
        parts = [zero, jnp.where(low, 0.0, turn(rows)), zero, jnp.where(low, 0.0, rows)]
    return jnp.stack(parts, axis=1).reshape(BLOCK, RHS)


def face_c(end):
    return pl.ds(3 * end, FACE, stride=4)


def fill_traces(lowered, inv_ref, tr_ref, app_ref):
    for e in range(ELEMS):
        field = lowered(e)
        applied = mm(inv_ref[e], field, TN)
        app_ref[e] = applied
        for end in range(2):
            tr_ref[6 * e + end] = trace_a(applied, end).astype(jnp.bfloat16)
            tr_ref[6 * e + 2 + end] = trace_b(applied, end).astype(jnp.bfloat16)
            tr_ref[6 * e + 4 + end] = app_ref[e, face_c(end), :].astype(jnp.bfloat16)


def list_slots(wanted, sign, list_ref, count_ref, slot_ref):
    live = count_ref[0, 0]

    def look(h, n):
        slot_ref[n] = h
        hit = jnp.logical_and(list_ref[2, h] * sign == wanted, h < live)
        return n + hit.astype(jnp.int32)

    n = lax.fori_loop(0, HANG, look, jnp.int32(0), unroll=8)
    for i in range(GROUP):
        slot_ref[n + i] = 0
    return n


def fetch_list(wanted, sign, list_hbm, list_ref, count_ref, slot_ref, sem):
    copy = pltpu.make_async_copy(list_hbm, list_ref, sem)
    copy.start()

    def listing():
        copy.wait()
        return list_slots(wanted, sign, list_ref, count_ref, slot_ref)

    return listing


def each_slot(n, slot_ref, hang_hbm, hang_ref, sems, act):
    @pl.loop(0, n)
    def _(k):
        act(pltpu.make_async_copy(hang_hbm.at[slot_ref[k]], hang_ref.at[k], sems.at[k]))


def add_slots(acc, n, list_ref, hang_ref, tr_ref, slot_ref):
    def work(first, size):
        parts = []
        for i in range(size):
            k = first + i
            h = slot_ref[k]
            source = list_ref[0, h] * 6 + list_ref[1, h]
            target = jnp.where(k < n, list_ref[3, h], ELEMS)
            parts.append((target, mm(hang_ref[k], tr_ref[source], TN)))
        for target, part in parts:
            acc[target] += part

    whole = (n + GROUP // 2 - 1) // GROUP

    @pl.loop(0, whole)
    def _(g):
        work(g * GROUP, GROUP)

    @pl.when(n > whole * GROUP)
    def _():
        work(whole * GROUP, GROUP // 2)


def core_and_row():
    return lax.axis_index("c"), lax.axis_index("x") % 2


def flux(weights, tr_ref, e, f):
    return mm(weights, tr_ref[6 * e + f], TN)


def swap_if(flag, a, b):
    return jnp.where(flag, b, a), jnp.where(flag, a, b)


def edge_fluxes(face_ref, tr_ref, ya_ref, yb_ref):
    _, odd = core_and_row()
    for x in range(2):
        for z in range(2):
            up = flux(face_ref[1, x, z], tr_ref, 4 * x + 2 + z, 3)
            down = flux(face_ref[2, x, z], tr_ref, 4 * x + z, 2)
            first, second = swap_if(odd == 1, up, down)
            ya_ref[2 * x + z] = first.astype(jnp.bfloat16)
            yb_ref[2 * x + z] = second.astype(jnp.bfloat16)


def cross_part(acc, out_refs, listing, side, list_ref, face_ref, hang_ref, tr_ref, slot_ref):
    for m in range(4):
        piece = flux(face_ref[0, m // 2, m % 2], tr_ref, m + 4 * side, side)
        acc[m + 4 * (1 - side)] = jnp.where(side == 1, spread_a(piece, 0), spread_a(piece, 1))
        acc[m + 4 * side] = jnp.zeros((BLOCK, RHS), jnp.float32)
    add_slots(acc, listing(), list_ref, hang_ref, tr_ref, slot_ref)
    for i, ref in enumerate(out_refs):
        size = ref.shape[0]
        ref[...] = acc[size * i : size * i + size].astype(ref.dtype)


def first_kernel(
    list_hbm, count_ref, rhs_hbm, inv_hbm, face_hbm, hang_hbm,
    rhs_ref, inv_ref, face_ref, hang_ref, tr_ref, cross_ref,
    acc, app_ref, list_ref, slot_ref, sems, hang_sems,
):
    core, _ = core_and_row()
    copies = []

    def bring(source, target):
        copies.append(pltpu.make_async_copy(source, target, sems.at[len(copies)]))
        copies[-1].start()

    bring(list_hbm, list_ref)
    for e in range(0, ELEMS, 2):
        pair = pl.ds(e, 2)
        bring(rhs_hbm.at[pair], rhs_ref.at[pair])
        bring(inv_hbm.at[pair], inv_ref.at[pair])
    late = len(copies)
    bring(face_hbm.at[core, :, :, core], face_ref.at[0])
    copies[0].wait()
    n = list_slots(1, 2 * core - 1, list_ref, count_ref, slot_ref)
    each_slot(n, slot_ref, hang_hbm, hang_ref, hang_sems, lambda copy: copy.start())

    def lowered(e):
        if e % 2 == 0:
            copies[e + 1].wait()
            copies[e + 2].wait()
        return rhs_ref[e]

    fill_traces(lowered, inv_ref, tr_ref, app_ref)
    for copy in copies[late:]:
        copy.wait()
    each_slot(n, slot_ref, hang_hbm, hang_ref, hang_sems, lambda copy: copy.wait())
    cross_part(acc, (cross_ref,), lambda: n, core, list_ref, face_ref, hang_ref, tr_ref, slot_ref)


def side_first_kernel(
    list_hbm, count_ref, face_hbm, hang_hbm, tr_ref, chip_ref, chip2_ref, ya_ref, yb_ref, face_ref, hang_ref, own_face_ref, own_hang_ref,
    acc, slot_ref, list_ref, list_sem, own_slot_ref, sems, hang_sems, own_hang_sems,
):
    core, _ = core_and_row()
    listing = fetch_list(-1, 2 * core - 1, list_hbm, list_ref, count_ref, slot_ref, list_sem)
    pieces = [
        face_hbm.at[1, :, :, 0], face_hbm.at[0, :, :, 1], face_hbm.at[:, 1, :, 2],
        face_hbm.at[:, 0, :, 3], face_hbm.at[:, :, 1, 4], face_hbm.at[:, :, 0, 5],
    ]
    mine = [face_hbm.at[1 - core, :, :, 1 - core], face_hbm.at[:, 1, :, 3], face_hbm.at[:, 0, :, 2]]
    copies = [pltpu.make_async_copy(p, face_ref.at[f], sems.at[6 + f]) for f, p in enumerate(mine)]
    copies += [pltpu.make_async_copy(p, own_face_ref.at[f], sems.at[f]) for f, p in enumerate(pieces)]
    for copy in copies[:3]:
        copy.start()
    n = listing()
    each_slot(n, slot_ref, hang_hbm, hang_ref, hang_sems, lambda copy: copy.start())
    for copy in copies[3:]:
        copy.start()
    own_n = list_slots(0, 1, list_ref, count_ref, own_slot_ref)
    each_slot(own_n, own_slot_ref, hang_hbm, own_hang_ref, own_hang_sems, lambda copy: copy.start())
    for copy in copies[:3]:
        copy.wait()
    edge_fluxes(face_ref, tr_ref, ya_ref, yb_ref)
    each_slot(n, slot_ref, hang_hbm, hang_ref, hang_sems, lambda copy: copy.wait())
    cross_part(acc, (chip_ref, chip2_ref), lambda: n, 1 - core, list_ref, face_ref, hang_ref, tr_ref, slot_ref)
    for copy in copies[3:]:
        copy.wait()
    each_slot(own_n, own_slot_ref, hang_hbm, own_hang_ref, own_hang_sems, lambda copy: copy.wait())


def side_second_kernel(
    list_hbm, count_ref, face_ref, hang_ref, tr_ref, chip_ref, chip2_ref, ya_ref, yb_ref, acc, slot_ref, list_ref, sem
):
    core, _ = core_and_row()
    listing = fetch_list(-1, 2 * core - 1, list_hbm, list_ref, count_ref, slot_ref, sem)
    edge_fluxes(face_ref, tr_ref, ya_ref, yb_ref)
    cross_part(acc, (chip_ref, chip2_ref), listing, 1 - core, list_ref, face_ref, hang_ref, tr_ref, slot_ref)


def own_part(listing, list_ref, face_ref, hang_ref, tr_ref, own_ref, acc, slot_ref):
    for e in range(ELEMS):
        x, y, z = (e >> 2) & 1, (e >> 1) & 1, e & 1
        from_x = flux(face_ref[x, y, z], tr_ref, e ^ 4, x)
        from_y = flux(face_ref[2 + y, x, z], tr_ref, e ^ 2, 2 + y)
        from_z = flux(face_ref[4 + z, x, y], tr_ref, e ^ 1, 4 + z)
        acc[e] = spread_a(from_x, 1 - x) + spread_b(from_y, 1 - y)
        acc[e, face_c(1 - z), :] += from_z
    add_slots(acc, listing(), list_ref, hang_ref, tr_ref, slot_ref)
    own_ref[...] = acc[0:ELEMS]


def own_kernel(list_hbm, count_ref, face_ref, hang_ref, tr_ref, own_ref, acc, slot_ref, list_ref, sem):
    listing = fetch_list(0, 1, list_hbm, list_ref, count_ref, slot_ref, sem)
    own_part(listing, list_ref, face_ref, hang_ref, tr_ref, own_ref, acc, slot_ref)


def inner(e, *pairs):
    return [jnp.sum((a[e].astype(jnp.float32) * b[e].astype(jnp.float32)).reshape(BLOCK // 8, 8, RHS), axis=0) for a, b in pairs]


def gram_rows(*pairs):
    totals = inner(0, *pairs)
    for e in range(1, ELEMS):
        totals = [t + p for t, p in zip(totals, inner(e, *pairs))]
    rows = [jnp.sum(t, axis=0, keepdims=True) for t in totals]
    return jnp.concatenate(rows, axis=1)


def own_gram_kernel(
    list_hbm, count_ref, face_ref, hang_ref, tr_ref, rhs_ref, w1_ref, own_ref, gram_ref, acc, slot_ref, list_ref, sem
):
    listing = fetch_list(0, 1, list_hbm, list_ref, count_ref, slot_ref, sem)
    own_part(listing, list_ref, face_ref, hang_ref, tr_ref, own_ref, acc, slot_ref)
    gram_ref[...] = gram_rows((rhs_ref, rhs_ref), (rhs_ref, w1_ref), (w1_ref, w1_ref))


def landed(e, own_ref, cross_ref, chip_refs, ya_ref, yb_ref):
    _, odd = core_and_row()
    y = (e >> 1) & 1
    n = 2 * (e >> 2) + (e & 1)
    edge = swap_if(odd == 1, ya_ref[n].astype(jnp.float32), yb_ref[n].astype(jnp.float32))[1 - y]
    came = cross_ref[e].astype(jnp.float32) + chip_refs[e // 4][e % 4].astype(jnp.float32)
    return own_ref[e] + came + spread_b(edge, y)


def near_kernel(own_ref, chip_ref, chip2_ref, ya_ref, yb_ref, near_ref):
    _, odd = core_and_row()
    for e in range(ELEMS):
        y = (e >> 1) & 1
        n = 2 * (e >> 2) + (e & 1)
        edge = swap_if(odd == 1, ya_ref[n].astype(jnp.float32), yb_ref[n].astype(jnp.float32))[1 - y]
        chip = (chip_ref, chip2_ref)[e // 4][e % 4].astype(jnp.float32)
        near_ref[e] = own_ref[e] + chip + spread_b(edge, y)


def second_kernel(
    list_hbm, count_ref, own_ref, in_cross, in_chip, in_chip2, in_ya, in_yb, inv_ref, face_ref, hang_ref,
    w_ref, tr_ref, cross_ref, acc, app_ref, slot_ref, list_ref, sem,
):
    core, _ = core_and_row()
    listing = fetch_list(1, 2 * core - 1, list_hbm, list_ref, count_ref, slot_ref, sem)

    def lowered(e):
        w = landed(e, own_ref, in_cross, (in_chip, in_chip2), in_ya, in_yb)
        w_ref[e] = w
        return w.astype(jnp.bfloat16)

    fill_traces(lowered, inv_ref, tr_ref, app_ref)
    cross_part(acc, (cross_ref,), listing, core, list_ref, face_ref, hang_ref, tr_ref, slot_ref)


def last_kernel(near_ref, in_cross, rhs_ref, w1_ref, early_ref, w_ref, keep_ref, give_ref):
    for e in range(ELEMS):
        w_ref[e] = near_ref[e] + in_cross[e].astype(jnp.float32)
    late = gram_rows((rhs_ref, w_ref), (w1_ref, w_ref), (w_ref, w_ref))
    early = early_ref[...]
    core, _ = core_and_row()
    keep_ref[...] = jnp.where(core == 0, early, late)
    give_ref[...] = jnp.where(core == 0, late, early)


def combine_kernel(entries, mine_ref, other_ref, rhs_ref, w1_ref, w2_ref, out_hbm, hess_ref, out_ref, sems):
    core, _ = core_and_row()
    mine = mine_ref[...] * (1.0 / entries)
    other = other_ref[...] * (1.0 / entries)
    early = jnp.where(core == 0, mine, other)
    late = jnp.where(core == 0, other, mine)
    g00, g01, g11 = (early[:, RHS * i : RHS * i + RHS] for i in range(3))
    g02, g12, g22 = (late[:, RHS * i : RHS * i + RHS] for i in range(3))
    norm0 = g00 + EPS
    size0 = jnp.sqrt(norm0)
    h11 = (g00 + g01) / norm0
    c1 = (EPS - g01) / norm0
    square1 = jnp.maximum(g11 + 2.0 * c1 * g01 + c1 * c1 * g00, 0.0) / norm0 + EPS
    h21 = jnp.sqrt(square1)
    s2 = 1.0 / (size0 * h21)
    ratio = (g02 + c1 * g01 + EPS * h11) / norm0
    h12 = ratio * s2 * size0
    q = EPS / square1 - s2 * s2 * (g12 + c1 * (g11 + g02 + c1 * g01))
    h22 = 1.0 - q
    alpha = c1 + q
    beta = c1 * q - ratio
    total = g22 + 2.0 * (alpha * g12 + beta * g02 + alpha * beta * g01)
    total = total + alpha * alpha * g11 + beta * beta * g00
    h32 = jnp.sqrt(s2 * s2 * jnp.maximum(total, 0.0) + EPS)
    zero = jnp.zeros_like(h11)
    for i, row in enumerate(((h11, h12), (h21, h22), (zero, h32))):
        hess_ref[i] = jnp.concatenate(row, axis=0)
    k2 = s2 / h32
    k1 = k2 * alpha
    k0 = k2 * beta
    copies = []
    for e in range(ELEMS):
        out_ref[e] = k2 * w2_ref[e] + k1 * w1_ref[e] + k0 * rhs_ref[e].astype(jnp.float32)
        copies.append(pltpu.make_async_copy(out_ref.at[e], out_hbm.at[e], sems.at[e]))
        copies[e].start()
    for copy in copies:
        copy.wait()


def shape(dims, dtype=jnp.float32):
    return jax.ShapeDtypeStruct(dims, dtype)


FIELD = (ELEMS, BLOCK, RHS)
TRACES = (6 * ELEMS, FACE, RHS)
SIDE = (4, FACE, RHS)
HALF = (4, BLOCK, RHS)
SMEM = pl.BlockSpec(memory_space=pltpu.SMEM)
VMEM = pl.BlockSpec(memory_space=pltpu.VMEM)
HBM = pl.BlockSpec(memory_space=pltpu.HBM)


def call(kernel, in_specs, outs, scratch, flops, moved, out_specs=None):
    return pl.pallas_call(
        kernel,
        out_shape=outs,
        in_specs=in_specs,
        out_specs=out_specs or [VMEM] * len(outs),
        scratch_shapes=scratch,
        compiler_params=pltpu.CompilerParams(vmem_limit_bytes=VMEM_LIMIT),
        cost_estimate=pl.CostEstimate(flops=flops, bytes_accessed=moved, transcendentals=0),
    )


def stay(x):
    return pltpu.with_memory_space_constraint(x, pltpu.HBM)


def per_device(entries, pairs, rhs_field, inv_block, face_block, hang_list, hang_count, hang_block):
    rows = stay(hang_list.reshape(HANG, 4).T)
    count = hang_count
    field = pltpu.VMEM(FIELD, jnp.float32)
    acc = pltpu.VMEM((ELEMS + 1, BLOCK, RHS), jnp.float32)
    slots = pltpu.SMEM((HANG + 8,), jnp.int32)
    bf16 = jnp.bfloat16
    million = 10**6
    later = [HBM, SMEM]
    lists = [slots, pltpu.SMEM((4, HANG), jnp.int32), pltpu.SemaphoreType.DMA]
    sems = lambda n: pltpu.SemaphoreType.DMA((n,))
    faces = stay(face_block)
    hangs = stay(hang_block.reshape(HANG, FACE, BLOCK))
    packed = shape((HANG, FACE, BLOCK), bf16)
    held = lambda n: shape((n, 2, 2, FACE, FACE), bf16)
    sent = [shape(TRACES, bf16), shape(FIELD, bf16)]
    beside = [shape(HALF, bf16)] * 2 + [shape(SIDE, bf16)] * 2

    rhs, inv, face, hang, traces, cross = call(
        first_kernel, [HBM, SMEM] + [HBM] * 4, [shape(FIELD, bf16), shape((ELEMS, BLOCK, BLOCK), bf16), held(1), packed] + sent,
        [
            acc, field, pltpu.SMEM((4, HANG), jnp.int32), slots,
            sems(ELEMS + 2), sems(HANG),
        ],
        300 * million, 6 * million,
    )(rows, count, stay(rhs_field.reshape(FIELD)), stay(inv_block.reshape(ELEMS, BLOCK, BLOCK)), faces, hangs)

    def exchange(cross, side_call, own_call):
        in_cross = lax.ppermute(cross, ("z", "y", "c"), pairs["cross"])
        low, high, ya, yb, *weights = side_call()
        in_ya = lax.ppermute(ya, "x", pairs["even"])
        in_yb = lax.ppermute(yb, "x", pairs["odd"])
        in_chip = [lax.ppermute(part, "c", [(0, 1), (1, 0)]) for part in (low, high)]
        own, *rest = own_call(weights[2:])
        return (own, in_cross, *in_chip, in_ya, in_yb), weights, rest

    def side_first():
        return call(
            side_first_kernel, later + [HBM, HBM, VMEM], beside + [held(3), packed, held(6), packed],
            [acc, *lists, slots, sems(9), sems(HANG), sems(HANG)], SIDE_FLOPS, 4 * million,
        )(rows, count, faces, hangs, traces)

    def own_first(weights):
        return call(own_kernel, later + [VMEM] * 3, [shape(FIELD)], [acc, *lists], OWN_FLOPS, 6 * million)(
            rows, count, *weights, traces
        )

    arrived, weights, _ = exchange(cross, side_first, own_first)
    w1, traces, cross = call(
        second_kernel, later + [VMEM] * 9, [shape(FIELD)] + sent, [acc, field, *lists], 300 * million, 8 * million,
    )(rows, count, *arrived, inv, face, hang)

    def side_second():
        return call(side_second_kernel, later + [VMEM] * 3, beside, [acc, *lists], SIDE_FLOPS, 4 * million)(
            rows, count, *weights[:2], traces
        )

    def own_second(_):
        return call(
            own_gram_kernel, later + [VMEM] * 5, [shape(FIELD), shape((1, 3 * RHS))], [acc, *lists],
            OWN_FLOPS, 6 * million,
        )(rows, count, *weights[2:], traces, rhs, w1)

    (own, in_cross, *others), _, (early,) = exchange(cross, side_second, own_second)
    near = call(near_kernel, [VMEM] * 5, [shape(FIELD)], [], NEAR_FLOPS, 6 * million)(own, *others)[0]
    w2, keep, give = call(
        last_kernel, [VMEM] * 5, [shape(FIELD), shape((1, 3 * RHS)), shape((1, 3 * RHS))], [], 10 * million, 8 * million
    )(near, in_cross, rhs, w1, early)

    swap = [(0, 1), (1, 0)]
    part = keep + lax.ppermute(give, "c", swap)
    chips = lax.axis_size(("z", "y", "x"))
    mine = lax.all_to_all(jnp.broadcast_to(part, (chips, 1, 3 * RHS)), ("z", "y", "x"), 0, 0).sum(0)
    last, hessenberg = call(
        functools.partial(combine_kernel, entries), [VMEM] * 5, [shape(FIELD), shape((3, 2, RHS))],
        [field, pltpu.SemaphoreType.DMA((ELEMS,))], 10 * million, 6 * million, [HBM, VMEM],
    )(mine, lax.ppermute(mine, "c", swap), rhs, w1, w2)
    return last.reshape(rhs_field.shape), hessenberg


def solution(mesh):
    count_x, count_y = mesh.shape["gx"], mesh.shape["gy"]
    grid = jax.sharding.Mesh(
        mesh.devices.reshape(CHIPS_Z, CHIPS_Y, 2, count_y), ("z", "y", "c", "x")
    )
    pairs = {"cross": [], "even": [], "odd": []}
    for i in range(1, count_x - 1, 2):
        pairs["cross"] += [(i, i + 1), (i + 1, i)]
    for j in range(count_y - 1):
        pairs["odd" if j % 2 else "even"] += [(j, j + 1), (j + 1, j)]
    long = ("z", "y", "c")
    in_specs = (P(long, "x"),) * 6
    out_specs = (P(long, "x"), P())
    entries = float(ELEMS * BLOCK * count_x * count_y)
    return jax.shard_map(
        functools.partial(per_device, entries, pairs),
        mesh=grid, in_specs=in_specs, out_specs=out_specs, check_vma=False,
    )
```

```python
import functools

import jax
import jax.numpy as jnp
from jax import lax
from jax.experimental import pallas as pl
from jax.experimental.pallas import tpu as pltpu
from jax.sharding import PartitionSpec as P

VARS = 5
CHIPS_Z = 8
CHIPS_Y = 4
BLOCK = 320
FACE = 80
ELEMS = 8
RHS = 128
HANG = 32
EPS = 1e-6
GROUP = 8
SIDE_FLOPS = 100 * 10**6
OWN_FLOPS = 4000 * 10**6
NEAR_FLOPS = 10**6
VMEM_LIMIT = 40 * 1024 * 1024

TN = (((0,), (0,)), ((), ()))
NN = (((1,), (0,)), ((), ()))


def mm(a, b, dims):
    return lax.dot_general(a, b, dims, preferred_element_type=jnp.float32)


def low_half():
    return lax.broadcasted_iota(jnp.int32, (10, 8, RHS), 1) < 4


def turn(x):
    return pltpu.roll(x, 4, 1)


def trace_a(field, end):
    return field.reshape(VARS, 4, 16, RHS)[:, 3 * end].reshape(FACE, RHS)


def trace_b(field, end):
    rows = field.reshape(10, 4, 8, RHS)
    if end == 0:
        out = jnp.where(low_half(), rows[:, 0], turn(rows[:, 2]))
    else:
        out = jnp.where(low_half(), turn(rows[:, 1]), rows[:, 3])
    return out.reshape(FACE, RHS)


def spread_a(values, end):
    piece = values.reshape(VARS, 1, 16, RHS)
    zero = jnp.zeros((VARS, 3, 16, RHS), jnp.float32)
    return jnp.concatenate([zero, piece] if end else [piece, zero], axis=1).reshape(BLOCK, RHS)


def spread_b(values, end):
    rows = values.reshape(10, 8, RHS)
    zero = jnp.zeros_like(rows)
    low = low_half()
    if end == 0:
        parts = [jnp.where(low, rows, 0.0), zero, jnp.where(low, turn(rows), 0.0), zero]
    else:
        parts = [zero, jnp.where(low, 0.0, turn(rows)), zero, jnp.where(low, 0.0, rows)]
    return jnp.stack(parts, axis=1).reshape(BLOCK, RHS)


def face_c(end):
    return pl.ds(3 * end, FACE, stride=4)


def fill_traces(lowered, inv_ref, tr_ref, app_ref):
    for e in range(ELEMS):
        field = lowered(e)
        applied = mm(inv_ref[e], field, TN)
        app_ref[e] = applied
        for end in range(2):
            tr_ref[6 * e + end] = trace_a(applied, end).astype(jnp.bfloat16)
            tr_ref[6 * e + 2 + end] = trace_b(applied, end).astype(jnp.bfloat16)
            tr_ref[6 * e + 4 + end] = app_ref[e, face_c(end), :].astype(jnp.bfloat16)


def list_slots(wanted, sign, list_ref, count_ref, slot_ref):
    live = count_ref[0, 0]

    def look(h, n):
        slot_ref[n] = h
        hit = jnp.logical_and(list_ref[2, h] * sign == wanted, h < live)
        return n + hit.astype(jnp.int32)

    n = lax.fori_loop(0, HANG, look, jnp.int32(0), unroll=8)
    for i in range(GROUP):
        slot_ref[n + i] = 0
    return n


def fetch_list(wanted, sign, list_hbm, list_ref, count_ref, slot_ref, sem):
    copy = pltpu.make_async_copy(list_hbm, list_ref, sem)
    copy.start()

    def listing():
        copy.wait()
        return list_slots(wanted, sign, list_ref, count_ref, slot_ref)

    return listing


def each_slot(n, slot_ref, hang_hbm, hang_ref, sems, act):
    @pl.loop(0, n)
    def _(k):
        act(pltpu.make_async_copy(hang_hbm.at[slot_ref[k]], hang_ref.at[k], sems.at[k]))


def add_slots(acc, n, list_ref, hang_ref, tr_ref, slot_ref):
    def work(first, size):
        parts = []
        for i in range(size):
            k = first + i
            h = slot_ref[k]
            source = list_ref[0, h] * 6 + list_ref[1, h]
            target = jnp.where(k < n, list_ref[3, h], ELEMS)
            parts.append((target, mm(hang_ref[k], tr_ref[source], TN)))
        for target, part in parts:
            acc[target] += part

    whole = (n + GROUP // 2 - 1) // GROUP

    @pl.loop(0, whole)
    def _(g):
        work(g * GROUP, GROUP)

    @pl.when(n > whole * GROUP)
    def _():
        work(whole * GROUP, GROUP // 2)


def core_and_row():
    return lax.axis_index("c"), lax.axis_index("x") % 2


def flux(weights, tr_ref, e, f):
    return mm(weights, tr_ref[6 * e + f], TN)


def swap_if(flag, a, b):
    return jnp.where(flag, b, a), jnp.where(flag, a, b)


def edge_fluxes(face_ref, tr_ref, ya_ref, yb_ref):
    _, odd = core_and_row()
    for x in range(2):
        for z in range(2):
            up = flux(face_ref[1, x, z], tr_ref, 4 * x + 2 + z, 3)
            down = flux(face_ref[2, x, z], tr_ref, 4 * x + z, 2)
            first, second = swap_if(odd == 1, up, down)
            ya_ref[2 * x + z] = first.astype(jnp.bfloat16)
            yb_ref[2 * x + z] = second.astype(jnp.bfloat16)


def cross_part(acc, out_refs, listing, side, list_ref, face_ref, hang_ref, tr_ref, slot_ref):
    for m in range(4):
        piece = flux(face_ref[0, m // 2, m % 2], tr_ref, m + 4 * side, side)
        acc[m + 4 * (1 - side)] = jnp.where(side == 1, spread_a(piece, 0), spread_a(piece, 1))
        acc[m + 4 * side] = jnp.zeros((BLOCK, RHS), jnp.float32)
    add_slots(acc, listing(), list_ref, hang_ref, tr_ref, slot_ref)
    for i, ref in enumerate(out_refs):
        size = ref.shape[0]
        ref[...] = acc[size * i : size * i + size].astype(ref.dtype)


def first_kernel(
    list_hbm, count_ref, rhs_hbm, inv_hbm, face_hbm, hang_hbm,
    rhs_ref, inv_ref, face_ref, hang_ref, tr_ref, cross_ref,
    acc, app_ref, list_ref, slot_ref, sems, hang_sems,
):
    core, _ = core_and_row()
    copies = []

    def bring(source, target):
        copies.append(pltpu.make_async_copy(source, target, sems.at[len(copies)]))
        copies[-1].start()

    bring(list_hbm, list_ref)
    for e in range(0, ELEMS, 2):
        pair = pl.ds(e, 2)
        bring(rhs_hbm.at[pair], rhs_ref.at[pair])
        bring(inv_hbm.at[pair], inv_ref.at[pair])
    late = len(copies)
    bring(face_hbm.at[core, :, :, core], face_ref.at[0])
    copies[0].wait()
    n = list_slots(1, 2 * core - 1, list_ref, count_ref, slot_ref)
    each_slot(n, slot_ref, hang_hbm, hang_ref, hang_sems, lambda copy: copy.start())

    def lowered(e):
        if e % 2 == 0:
            copies[e + 1].wait()
            copies[e + 2].wait()
        return rhs_ref[e]

    fill_traces(lowered, inv_ref, tr_ref, app_ref)
    for copy in copies[late:]:
        copy.wait()
    each_slot(n, slot_ref, hang_hbm, hang_ref, hang_sems, lambda copy: copy.wait())
    cross_part(acc, (cross_ref,), lambda: n, core, list_ref, face_ref, hang_ref, tr_ref, slot_ref)


def side_first_kernel(
    list_hbm, count_ref, face_hbm, hang_hbm, tr_ref, chip_ref, chip2_ref, ya_ref, yb_ref, face_ref, hang_ref,
    acc, slot_ref, list_ref, list_sem, sems, hang_sems,
):
    core, _ = core_and_row()
    listing = fetch_list(-1, 2 * core - 1, list_hbm, list_ref, count_ref, slot_ref, list_sem)
    mine = [face_hbm.at[1 - core, :, :, 1 - core], face_hbm.at[:, 1, :, 3], face_hbm.at[:, 0, :, 2]]
    copies = [pltpu.make_async_copy(p, face_ref.at[f], sems.at[f]) for f, p in enumerate(mine)]
    for copy in copies:
        copy.start()
    n = listing()
    each_slot(n, slot_ref, hang_hbm, hang_ref, hang_sems, lambda copy: copy.start())
    for copy in copies:
        copy.wait()
    edge_fluxes(face_ref, tr_ref, ya_ref, yb_ref)
    each_slot(n, slot_ref, hang_hbm, hang_ref, hang_sems, lambda copy: copy.wait())
    cross_part(acc, (chip_ref, chip2_ref), lambda: n, 1 - core, list_ref, face_ref, hang_ref, tr_ref, slot_ref)


def side_second_kernel(
    list_hbm, count_ref, face_ref, hang_ref, tr_ref, chip_ref, chip2_ref, ya_ref, yb_ref, acc, slot_ref, list_ref, sem
):
    core, _ = core_and_row()
    listing = fetch_list(-1, 2 * core - 1, list_hbm, list_ref, count_ref, slot_ref, sem)
    edge_fluxes(face_ref, tr_ref, ya_ref, yb_ref)
    cross_part(acc, (chip_ref, chip2_ref), listing, 1 - core, list_ref, face_ref, hang_ref, tr_ref, slot_ref)


def own_part(listing, list_ref, face_ref, hang_ref, tr_ref, own_ref, acc, slot_ref):
    for e in range(ELEMS):
        x, y, z = (e >> 2) & 1, (e >> 1) & 1, e & 1
        from_x = flux(face_ref[x, y, z], tr_ref, e ^ 4, x)
        from_y = flux(face_ref[2 + y, x, z], tr_ref, e ^ 2, 2 + y)
        from_z = flux(face_ref[4 + z, x, y], tr_ref, e ^ 1, 4 + z)
        acc[e] = spread_a(from_x, 1 - x) + spread_b(from_y, 1 - y)
        acc[e, face_c(1 - z), :] += from_z
    add_slots(acc, listing(), list_ref, hang_ref, tr_ref, slot_ref)
    own_ref[...] = acc[0:ELEMS]


def own_kernel(
    list_hbm, count_ref, face_hbm, hang_hbm, tr_ref, own_ref, face_ref, hang_ref,
    acc, slot_ref, list_ref, list_sem, sems, hang_sems,
):
    listing = fetch_list(0, 1, list_hbm, list_ref, count_ref, slot_ref, list_sem)
    pieces = [
        face_hbm.at[1, :, :, 0], face_hbm.at[0, :, :, 1], face_hbm.at[:, 1, :, 2],
        face_hbm.at[:, 0, :, 3], face_hbm.at[:, :, 1, 4], face_hbm.at[:, :, 0, 5],
    ]
    copies = [pltpu.make_async_copy(p, face_ref.at[f], sems.at[f]) for f, p in enumerate(pieces)]
    for copy in copies:
        copy.start()
    n = listing()
    each_slot(n, slot_ref, hang_hbm, hang_ref, hang_sems, lambda copy: copy.start())
    for copy in copies:
        copy.wait()

    def brought():
        each_slot(n, slot_ref, hang_hbm, hang_ref, hang_sems, lambda copy: copy.wait())
        return n

    own_part(brought, list_ref, face_ref, hang_ref, tr_ref, own_ref, acc, slot_ref)


def inner(e, *pairs):
    return [jnp.sum((a[e].astype(jnp.float32) * b[e].astype(jnp.float32)).reshape(BLOCK // 8, 8, RHS), axis=0) for a, b in pairs]


def gram_rows(*pairs):
    totals = inner(0, *pairs)
    for e in range(1, ELEMS):
        totals = [t + p for t, p in zip(totals, inner(e, *pairs))]
    rows = [jnp.sum(t, axis=0, keepdims=True) for t in totals]
    return jnp.concatenate(rows, axis=1)


def own_gram_kernel(
    list_hbm, count_ref, face_ref, hang_ref, tr_ref, rhs_ref, w1_ref, own_ref, gram_ref, acc, slot_ref, list_ref, sem
):
    listing = fetch_list(0, 1, list_hbm, list_ref, count_ref, slot_ref, sem)
    own_part(listing, list_ref, face_ref, hang_ref, tr_ref, own_ref, acc, slot_ref)
    gram_ref[...] = gram_rows((rhs_ref, rhs_ref), (rhs_ref, w1_ref), (w1_ref, w1_ref))


def landed(e, own_ref, cross_ref, chip_refs, ya_ref, yb_ref):
    _, odd = core_and_row()
    y = (e >> 1) & 1
    n = 2 * (e >> 2) + (e & 1)
    edge = swap_if(odd == 1, ya_ref[n].astype(jnp.float32), yb_ref[n].astype(jnp.float32))[1 - y]
    came = cross_ref[e].astype(jnp.float32) + chip_refs[e // 4][e % 4].astype(jnp.float32)
    return own_ref[e] + came + spread_b(edge, y)


def near_kernel(own_ref, chip_ref, chip2_ref, ya_ref, yb_ref, near_ref):
    _, odd = core_and_row()
    for e in range(ELEMS):
        y = (e >> 1) & 1
        n = 2 * (e >> 2) + (e & 1)
        edge = swap_if(odd == 1, ya_ref[n].astype(jnp.float32), yb_ref[n].astype(jnp.float32))[1 - y]
        chip = (chip_ref, chip2_ref)[e // 4][e % 4].astype(jnp.float32)
        near_ref[e] = own_ref[e] + chip + spread_b(edge, y)


def second_kernel(
    list_hbm, count_ref, own_ref, in_cross, in_chip, in_chip2, in_ya, in_yb, inv_ref, face_ref, hang_ref,
    w_ref, tr_ref, cross_ref, acc, app_ref, slot_ref, list_ref, sem,
):
    core, _ = core_and_row()
    listing = fetch_list(1, 2 * core - 1, list_hbm, list_ref, count_ref, slot_ref, sem)

    def lowered(e):
        w = landed(e, own_ref, in_cross, (in_chip, in_chip2), in_ya, in_yb)
        w_ref[e] = w
        return w.astype(jnp.bfloat16)

    fill_traces(lowered, inv_ref, tr_ref, app_ref)
    cross_part(acc, (cross_ref,), listing, core, list_ref, face_ref, hang_ref, tr_ref, slot_ref)


def last_kernel(near_ref, in_cross, rhs_ref, w1_ref, early_ref, w_ref, keep_ref, give_ref):
    for e in range(ELEMS):
        w_ref[e] = near_ref[e] + in_cross[e].astype(jnp.float32)
    late = gram_rows((rhs_ref, w_ref), (w1_ref, w_ref), (w_ref, w_ref))
    early = early_ref[...]
    core, _ = core_and_row()
    keep_ref[...] = jnp.where(core == 0, early, late)
    give_ref[...] = jnp.where(core == 0, late, early)


def combine_kernel(entries, mine_ref, other_ref, rhs_ref, w1_ref, w2_ref, out_hbm, hess_ref, out_ref, sems):
    core, _ = core_and_row()
    mine = mine_ref[...] * (1.0 / entries)
    other = other_ref[...] * (1.0 / entries)
    early = jnp.where(core == 0, mine, other)
    late = jnp.where(core == 0, other, mine)
    g00, g01, g11 = (early[:, RHS * i : RHS * i + RHS] for i in range(3))
    g02, g12, g22 = (late[:, RHS * i : RHS * i + RHS] for i in range(3))
    norm0 = g00 + EPS
    size0 = jnp.sqrt(norm0)
    h11 = (g00 + g01) / norm0
    c1 = (EPS - g01) / norm0
    square1 = jnp.maximum(g11 + 2.0 * c1 * g01 + c1 * c1 * g00, 0.0) / norm0 + EPS
    h21 = jnp.sqrt(square1)
    s2 = 1.0 / (size0 * h21)
    ratio = (g02 + c1 * g01 + EPS * h11) / norm0
    h12 = ratio * s2 * size0
    q = EPS / square1 - s2 * s2 * (g12 + c1 * (g11 + g02 + c1 * g01))
    h22 = 1.0 - q
    alpha = c1 + q
    beta = c1 * q - ratio
    total = g22 + 2.0 * (alpha * g12 + beta * g02 + alpha * beta * g01)
    total = total + alpha * alpha * g11 + beta * beta * g00
    h32 = jnp.sqrt(s2 * s2 * jnp.maximum(total, 0.0) + EPS)
    zero = jnp.zeros_like(h11)
    for i, row in enumerate(((h11, h12), (h21, h22), (zero, h32))):
        hess_ref[i] = jnp.concatenate(row, axis=0)
    k2 = s2 / h32
    k1 = k2 * alpha
    k0 = k2 * beta
    copies = []
    for e in range(ELEMS):
        out_ref[e] = k2 * w2_ref[e] + k1 * w1_ref[e] + k0 * rhs_ref[e].astype(jnp.float32)
        copies.append(pltpu.make_async_copy(out_ref.at[e], out_hbm.at[e], sems.at[e]))
        copies[e].start()
    for copy in copies:
        copy.wait()


def shape(dims, dtype=jnp.float32):
    return jax.ShapeDtypeStruct(dims, dtype)


FIELD = (ELEMS, BLOCK, RHS)
TRACES = (6 * ELEMS, FACE, RHS)
SIDE = (4, FACE, RHS)
HALF = (4, BLOCK, RHS)
SMEM = pl.BlockSpec(memory_space=pltpu.SMEM)
VMEM = pl.BlockSpec(memory_space=pltpu.VMEM)
HBM = pl.BlockSpec(memory_space=pltpu.HBM)


def call(kernel, in_specs, outs, scratch, flops, moved, out_specs=None):
    return pl.pallas_call(
        kernel,
        out_shape=outs,
        in_specs=in_specs,
        out_specs=out_specs or [VMEM] * len(outs),
        scratch_shapes=scratch,
        compiler_params=pltpu.CompilerParams(vmem_limit_bytes=VMEM_LIMIT),
        cost_estimate=pl.CostEstimate(flops=flops, bytes_accessed=moved, transcendentals=0),
    )


def stay(x):
    return pltpu.with_memory_space_constraint(x, pltpu.HBM)


def per_device(entries, pairs, rhs_field, inv_block, face_block, hang_list, hang_count, hang_block):
    rows = stay(hang_list.reshape(HANG, 4).T)
    count = hang_count
    field = pltpu.VMEM(FIELD, jnp.float32)
    acc = pltpu.VMEM((ELEMS + 1, BLOCK, RHS), jnp.float32)
    slots = pltpu.SMEM((HANG + 8,), jnp.int32)
    bf16 = jnp.bfloat16
    million = 10**6
    later = [HBM, SMEM]
    lists = [slots, pltpu.SMEM((4, HANG), jnp.int32), pltpu.SemaphoreType.DMA]
    sems = lambda n: pltpu.SemaphoreType.DMA((n,))
    faces = stay(face_block)
    hangs = stay(hang_block.reshape(HANG, FACE, BLOCK))
    packed = shape((HANG, FACE, BLOCK), bf16)
    held = lambda n: shape((n, 2, 2, FACE, FACE), bf16)
    sent = [shape(TRACES, bf16), shape(FIELD, bf16)]
    beside = [shape(HALF, bf16)] * 2 + [shape(SIDE, bf16)] * 2

    rhs, inv, face, hang, traces, cross = call(
        first_kernel, [HBM, SMEM] + [HBM] * 4, [shape(FIELD, bf16), shape((ELEMS, BLOCK, BLOCK), bf16), held(1), packed] + sent,
        [
            acc, field, pltpu.SMEM((4, HANG), jnp.int32), slots,
            sems(ELEMS + 2), sems(HANG),
        ],
        300 * million, 6 * million,
    )(rows, count, stay(rhs_field.reshape(FIELD)), stay(inv_block.reshape(ELEMS, BLOCK, BLOCK)), faces, hangs)

    def exchange(cross, side_call, own_call):
        in_cross = lax.ppermute(cross, ("z", "y", "c"), pairs["cross"])
        low, high, ya, yb, *weights = side_call()
        in_ya = lax.ppermute(ya, "x", pairs["even"])
        in_yb = lax.ppermute(yb, "x", pairs["odd"])
        in_chip = [lax.ppermute(part, "c", [(0, 1), (1, 0)]) for part in (low, high)]
        own, *rest = own_call()
        return (own, in_cross, *in_chip, in_ya, in_yb), weights, rest

    def side_first():
        return call(
            side_first_kernel, later + [HBM, HBM, VMEM], beside + [held(3), packed],
            [acc, *lists, sems(3), sems(HANG)], SIDE_FLOPS, 4 * million,
        )(rows, count, faces, hangs, traces)

    def own_first():
        return call(
            own_kernel, later + [HBM, HBM, VMEM], [shape(FIELD), held(6), packed],
            [acc, *lists, sems(6), sems(HANG)], OWN_FLOPS, 6 * million,
        )(rows, count, faces, hangs, traces)

    arrived, weights, own_weights = exchange(cross, side_first, own_first)
    w1, traces, cross = call(
        second_kernel, later + [VMEM] * 9, [shape(FIELD)] + sent, [acc, field, *lists], 300 * million, 8 * million,
    )(rows, count, *arrived, inv, face, hang)

    def side_second():
        return call(side_second_kernel, later + [VMEM] * 3, beside, [acc, *lists], SIDE_FLOPS, 4 * million)(
            rows, count, *weights, traces
        )

    def own_second():
        return call(
            own_gram_kernel, later + [VMEM] * 5, [shape(FIELD), shape((1, 3 * RHS))], [acc, *lists],
            OWN_FLOPS, 6 * million,
        )(rows, count, *own_weights, traces, rhs, w1)

    (own, in_cross, *others), _, (early,) = exchange(cross, side_second, own_second)
    near = call(near_kernel, [VMEM] * 5, [shape(FIELD)], [], NEAR_FLOPS, 6 * million)(own, *others)[0]
    w2, keep, give = call(
        last_kernel, [VMEM] * 5, [shape(FIELD), shape((1, 3 * RHS)), shape((1, 3 * RHS))], [], 10 * million, 8 * million
    )(near, in_cross, rhs, w1, early)

    swap = [(0, 1), (1, 0)]
    part = keep + lax.ppermute(give, "c", swap)
    chips = lax.axis_size(("z", "y", "x"))
    mine = lax.all_to_all(jnp.broadcast_to(part, (chips, 1, 3 * RHS)), ("z", "y", "x"), 0, 0).sum(0)
    last, hessenberg = call(
        functools.partial(combine_kernel, entries), [VMEM] * 5, [shape(FIELD), shape((3, 2, RHS))],
        [field, pltpu.SemaphoreType.DMA((ELEMS,))], 10 * million, 6 * million, [HBM, VMEM],
    )(mine, lax.ppermute(mine, "c", swap), rhs, w1, w2)
    return last.reshape(rhs_field.shape), hessenberg


def solution(mesh):
    count_x, count_y = mesh.shape["gx"], mesh.shape["gy"]
    grid = jax.sharding.Mesh(
        mesh.devices.reshape(CHIPS_Z, CHIPS_Y, 2, count_y), ("z", "y", "c", "x")
    )
    pairs = {"cross": [], "even": [], "odd": []}
    for i in range(1, count_x - 1, 2):
        pairs["cross"] += [(i, i + 1), (i + 1, i)]
    for j in range(count_y - 1):
        pairs["odd" if j % 2 else "even"] += [(j, j + 1), (j + 1, j)]
    long = ("z", "y", "c")
    in_specs = (P(long, "x"),) * 6
    out_specs = (P(long, "x"), P())
    entries = float(ELEMS * BLOCK * count_x * count_y)
    return jax.shard_map(
        functools.partial(per_device, entries, pairs),
        mesh=grid, in_specs=in_specs, out_specs=out_specs, check_vma=False,
    )
```
